128 devices in a mesh: ctx: 32 (over z, y_lo, x), kv: 4 (over y_hi, core).
Axes of the slice: x: 4, y: 4 (y_hi: 2, y_lo: 2; y = y_hi * 2 + y_lo), z: 4, core: 2. Of those that a mesh axis runs over, the one named last changes fastest.
Arguments:
- queries: bfloat16 [16384, 4096], P('ctx', 'kv'), may hold values from -6 to 6
- keys: bfloat16 [16384, 1024], P('ctx', 'kv'), may hold values from -6 to 6
- values: bfloat16 [16384, 1024], P('ctx', 'kv'), may hold values from -24 to 24
- doc_lengths: int32 [16], replicated, may hold values from 1 to 12288, 16384 in all
- out_weight: bfloat16 [4096, 4096], P('kv'), may hold values from -0.375 to 0.375
Outputs:
- output: bfloat16 [16384, 4096], P(('ctx', 'kv'))
The draws below stay inside these ranges and needn't reach their ends.
Inputs may be any that keep to these rules, and one draw needn't show every extreme that they name: `doc_lengths`: whole documents laid end to end that fill all 16384 positions; the longest has exactly 12288 tokens.
All inputs are finite; a program needn't handle non-finite values.
Results may differ from the reference program's by a relative error of at most 0.015.
Values may be sent and summed in bfloat16 or wider, within the bound.
No kernel may reach another device: no remote copies, remote signals or barrier semaphores. Data moves between devices by JAX's collectives and lax.ppermute only.
A program may use at most 192 MiB of HBM per device.

```python
import math
import jax
import jax.numpy as jnp
import numpy as np
from jax import lax

D = 4096
QUERY_HEADS = 32
KEY_VALUE_HEADS = 8
HEAD_WIDTH = 128
DOCS = 16
PACKED_TOKENS = 16384
MOST = 12288


def draw_queries(key, part):
    random_seed_key = jax.random.fold_in(key, 21)
    final_output = 1.4 * jax.random.truncated_normal(random_seed_key, -4.0, 4.0, (PACKED_TOKENS, QUERY_HEADS * HEAD_WIDTH), jnp.float32)
    return final_output.astype(jnp.bfloat16)


def draw_keys(key, part):
    random_seed_key = jax.random.fold_in(key, 22)
    final_output = 1.4 * jax.random.truncated_normal(random_seed_key, -4.0, 4.0, (PACKED_TOKENS, KEY_VALUE_HEADS * HEAD_WIDTH), jnp.float32)
    return final_output.astype(jnp.bfloat16)


def block_levels(rng, extent, cuts, low, top_value):
    def one(axis_at, blocks):
        draws = jax.random.uniform(jax.random.fold_in(jax.random.fold_in(rng, 6), axis_at), (blocks,), jnp.float32, low / len(cuts), top_value / len(cuts))
        return jnp.repeat(jnp.exp(draws), extent[axis_at] // blocks).reshape((-1,) + (1,) * (len(extent) - axis_at - 1))

    loudness = one(*cuts[0])
    for cut in cuts[1:]:
        loudness = loudness * one(*cut)
    return loudness


def split_up(count, total, limit, skew):
    loads = [(1 << 20) // math.isqrt(standing ** skew) + 1 for standing in range(2, count + 1)]
    surplus, counts = total - limit - (count - 1), [1] * (count - 1)
    while surplus > 0:
        candidates = [i for i in range(count - 1) if counts[i] < limit]
        whole, budget = sum([loads[i] for i in candidates]), surplus
        for i in candidates:
            addition = min(limit - counts[i], max(1, budget * loads[i] // whole), surplus)
            counts[i] = counts[i] + addition
            surplus = surplus - addition
    return np.array([limit] + counts)


def uneven(stream_key, number_of, total, bound, lean):
    if number_of == 2:
        one = jax.random.randint(stream_key, (), max(1, total - bound), min(bound, total - 1) + 1)
        return jnp.stack([one, total - one])
    sizes = jnp.asarray(split_up(number_of, total, bound, lean), jnp.int32)
    pairs = (number_of - 1) // 2
    giver, taker = sizes[1:1 + 2 * pairs:2], sizes[2:2 + 2 * pairs:2]
    margin = jnp.minimum(giver - 1, bound - taker)
    shifted = jax.random.randint(jax.random.fold_in(stream_key, 1), (pairs,), 0, 1 << 20) % (margin + 1)
    sizes = sizes.at[1:1 + 2 * pairs:2].set(giver - shifted).at[2:2 + 2 * pairs:2].set(taker + shifted)
    return sizes[jax.random.permutation(jax.random.fold_in(stream_key, 2), number_of)]


def normal_values(rng, dims, spread, bound, split=(), kind=jnp.bfloat16):
    entries = jax.random.normal(rng, dims, jnp.float32) * spread
    if len(split) > 0:
        entries = block_levels(rng, dims, split, -0.22, 0.18) * entries
    return jnp.clip(entries, min=-bound, max=bound).astype(kind)


def setup_inputs(seed: int = 0) -> dict:
    key_of = jax.random.split(jax.random.key(seed), 6)
    queries = draw_queries(jax.random.fold_in(key_of[5], 71), 0)
    keys = draw_keys(jax.random.fold_in(key_of[5], 71), 0)
    values = normal_values(key_of[2], (PACKED_TOKENS, KEY_VALUE_HEADS * HEAD_WIDTH), 4.0, 24.0, ((0, 32), (1, 4)))
    doc_lengths = uneven(key_of[3], DOCS, PACKED_TOKENS, MOST, 2).astype(jnp.int32)
    out_weight = normal_values(key_of[4], (QUERY_HEADS * HEAD_WIDTH, D), (QUERY_HEADS * HEAD_WIDTH // 16) ** -0.5, 0.375, ((0, 4),))
    return dict(queries=queries, keys=keys, values=values, doc_lengths=doc_lengths, out_weight=out_weight)


def reference(queries, keys, values, doc_lengths, out_weight):
    group_width = QUERY_HEADS // KEY_VALUE_HEADS
    score_scale = HEAD_WIDTH ** -0.5
    doc_ends = jnp.cumsum(doc_lengths).astype(jnp.int32)
    positions = jnp.arange(PACKED_TOKENS, dtype=jnp.int32)
    segments = jnp.sum((doc_ends[None, :] <= positions[:, None]).astype(jnp.int32), axis=1)
    block_of_rows = min(512, PACKED_TOKENS)
    pieces = []
    for begin_row in range(0, PACKED_TOKENS, block_of_rows):
        finish_row = begin_row + block_of_rows
        query_slice = queries[begin_row:finish_row].astype(jnp.float32).reshape(block_of_rows, KEY_VALUE_HEADS, group_width, HEAD_WIDTH)
        key_slice = keys[:finish_row].astype(jnp.float32).reshape(finish_row, KEY_VALUE_HEADS, HEAD_WIDTH)
        value_slice = values[:finish_row].astype(jnp.float32).reshape(finish_row, KEY_VALUE_HEADS, HEAD_WIDTH)
        allowed = (segments[:finish_row][None, :] == segments[begin_row:finish_row][:, None]) & (
            positions[:finish_row][None, :] <= positions[begin_row:finish_row][:, None])

        def per_head(head_items):
            query_head, key_head, value_head = head_items
            scores = jnp.einsum("qgd,kd->gqk", query_head, key_head) * score_scale
            masked = jnp.where(allowed[None], scores, -1.0e30)
            row_top = jnp.max(masked, axis=-1, keepdims=True)
            weights = jnp.where(allowed[None], jnp.exp(masked - row_top), 0.0)
            row_total = jnp.sum(weights, axis=-1)
            rounded = lax.optimization_barrier(weights.astype(jnp.bfloat16)).astype(jnp.float32)
            blended = jnp.einsum("gqk,kd->qgd", rounded, value_head)
            return blended / jnp.transpose(row_total)[..., None]

        head_out = lax.map(per_head, (jnp.transpose(query_slice, (1, 0, 2, 3)),
                                      jnp.transpose(key_slice, (1, 0, 2)),
                                      jnp.transpose(value_slice, (1, 0, 2))))
        pieces.append(jnp.transpose(head_out, (1, 0, 2, 3)).reshape(block_of_rows, QUERY_HEADS * HEAD_WIDTH).astype(jnp.bfloat16))
    attended = jnp.concatenate(pieces, axis=0)
    return jnp.dot(attended, out_weight, preferred_element_type=jnp.float32).astype(jnp.bfloat16)
```

```python
import functools
import math

import jax
import jax.numpy as jnp
from jax import lax
from jax.experimental import pallas as pl
from jax.experimental.pallas import tpu as pltpu
from jax.sharding import PartitionSpec as P

HEAD_WIDTH = 128
NEG = -1e30
AXES = ("ctx", "kv")
SCALE2 = HEAD_WIDTH ** -0.5 * math.log2(math.e)
HALF = 256


def device_at(z, y_hi, y_lo, x, c):
    return ((z % 4) * 8 + y_lo * 4 + x % 4) * 4 + y_hi * 2 + c


def permutation(move):
    pairs = []
    for i in range(128):
        ctx, kv = divmod(i, 4)
        pairs.append((i, device_at(*move(ctx // 8, kv // 2, ctx // 4 % 2, ctx % 4, kv % 2))))
    return pairs


X_UP = permutation(lambda z, yh, yl, x, c: (z, yh, yl, x + 1, c))
X_DOWN = permutation(lambda z, yh, yl, x, c: (z, yh, yl, x + 3, c))
Y_LO = permutation(lambda z, yh, yl, x, c: (z, yh, 1 - yl, x, c))
Y_HI = permutation(lambda z, yh, yl, x, c: (z, 1 - yh, yl, x, c))
CORE = permutation(lambda z, yh, yl, x, c: (z, yh, yl, x, 1 - c))
TO_HEAD = [
    permutation(lambda z, yh, yl, x, c, k=k: (2 * c + (z ^ k) // 2, yh, yl, x, (z ^ k) % 2))
    for k in range(4)
]
TO_HOME = [[(b, a) for a, b in pairs] for pairs in TO_HEAD]


def send(x, pairs):
    return lax.ppermute(x, AXES, pairs)


def dot_nt(a, b):
    return lax.dot_general(a, b, (((1,), (1,)), ((), ())), preferred_element_type=jnp.float32)


def attention_kernel(first, last, info_ref, ends_ref, lo_ref, hi_ref, q_ref, mine_ref, other_ref, *refs):
    if first:
        acc_in = m_in = l_in = None
    else:
        acc_in, m_in, l_in = refs[:3]
        refs = refs[3:]
    if last:
        out_ref, acc, m_s, l_s, start_s = refs
    else:
        acc_out, m_out, l_out, acc, m_s, l_s, start_s = refs
    own_j = info_ref[4]
    core = info_ref[5]

    def q_block(qb, carry):
        zq = qb // 2
        hq = qb % 2
        gq = (zq * 8 + own_j) * 2 + hq
        rows = pl.ds(pl.multiple_of(qb * HALF, HALF), HALF)
        q_pos = gq * HALF + lax.broadcasted_iota(jnp.int32, (HALF, 128), 0)
        start = jnp.zeros((HALF, 128), jnp.int32)
        for doc in range(16):
            end = ends_ref[doc]
            start = jnp.maximum(start, jnp.where(q_pos >= end, end, 0))
        start_s[...] = start
        if first:
            acc[...] = jnp.zeros_like(acc)
            m_s[...] = jnp.full_like(m_s, NEG)
            l_s[...] = jnp.zeros_like(l_s)
        else:
            acc[...] = acc_in[rows, :]
            m_s[...] = m_in[rows, :]
            l_s[...] = l_in[rows, :]
        lo = lo_ref[gq]
        hi = hi_ref[gq]

        def update(slot, zk, gk, masked):
            k_all = jnp.concatenate([mine_ref[slot, zk, :, :128], other_ref[slot, zk, :, :128]], axis=0)
            v_all = jnp.concatenate([mine_ref[slot, zk, :, 128:], other_ref[slot, zk, :, 128:]], axis=0)
            if masked:
                column = lax.broadcasted_iota(jnp.int32, (HALF, 2 * HALF), 1)
                k_pos = gk * (2 * HALF) + jnp.where(core == 0, column, column ^ HALF)
                q_at = gq * HALF + lax.broadcasted_iota(jnp.int32, (HALF, 2 * HALF), 0)
                allowed = (k_pos <= q_at) & (k_pos >= start_s[:, :1])
            for h in range(2):
                cols = slice(h * 128, (h + 1) * 128)
                s = dot_nt(q_ref[rows, cols], k_all)
                if masked:
                    s = jnp.where(allowed, s, NEG)
                m_old = m_s[:, cols]
                m_new = jnp.maximum(m_old, jnp.max(s, axis=1, keepdims=True))
                shrink = jnp.exp2((m_old - m_new) * SCALE2)
                p = jnp.exp2((s - m_new[:, :1]) * SCALE2)
                if masked:
                    p = jnp.where(allowed, p, 0.0)
                m_s[:, cols] = m_new
                l_s[:, cols] = l_s[:, cols] * shrink + jnp.sum(p, axis=1, keepdims=True)
                acc[:, cols] = acc[:, cols] * shrink + jnp.dot(
                    p.astype(jnp.bfloat16), v_all, preferred_element_type=jnp.float32
                )

        def k_block(kb, carry):
            slot = kb // 4
            zk = kb % 4
            gk = zk * 8 + info_ref[slot]
            needed = (gk * 512 <= gq * HALF + HALF - 1) & (gk * 512 + 511 >= lo)
            full = (gk * 512 + 511 <= gq * HALF) & (gk * 512 >= hi)

            @pl.when(full)
            def _():
                update(slot, zk, gk, False)

            @pl.when(needed & jnp.logical_not(full))
            def _():
                update(slot, zk, gk, True)

            return carry

        lax.fori_loop(0, 16, k_block, 0)
        if last:
            out_ref[rows, :] = (acc[...] / l_s[...]).astype(jnp.bfloat16)
        else:
            acc_out[rows, :] = acc[...]
            m_out[rows, :] = m_s[...]
            l_out[rows, :] = l_s[...]
        return carry

    lax.fori_loop(0, 8, q_block, 0)


def attention(first, last, info, ends, lo, hi, q, mine, other, state):
    rows = q.shape[0]
    whole = pl.BlockSpec(memory_space=pltpu.VMEM)
    scalar = pl.BlockSpec(memory_space=pltpu.SMEM)
    wide = jax.ShapeDtypeStruct((rows, 256), jnp.float32)
    return pl.pallas_call(
        functools.partial(attention_kernel, first, last),
        out_shape=jax.ShapeDtypeStruct((rows, 256), jnp.bfloat16) if last else (wide, wide, wide),
        in_specs=[scalar] * 4 + [whole] * (3 if first else 6),
        out_specs=whole if last else (whole, whole, whole),
        scratch_shapes=[pltpu.VMEM((HALF, 256), jnp.float32)] * 3 + [pltpu.VMEM((HALF, 128), jnp.int32)],
        compiler_params=pltpu.CompilerParams(vmem_limit_bytes=50 * 1024 * 1024),
        cost_estimate=pl.CostEstimate(
            flops=12_000_000_000, bytes_accessed=8 * 1024 * 1024, transcendentals=12_000_000
        ),
        name="attend_last" if last else "attend_first",
    )(info, ends, lo, hi, q, mine, other, *state)


def pick(stacked, index):
    return lax.dynamic_index_in_dim(stacked, index, 0, keepdims=False)


def on_device(queries, keys, values, doc_lengths, out_weight):
    ctx = lax.axis_index("ctx")
    kv = lax.axis_index("kv")
    z, y_lo, x = ctx // 8, ctx // 4 % 2, ctx % 4
    y_hi, core = kv // 2, kv % 2
    j = ctx % 8
    mine_d = 2 * (z % 2) + core
    ends = jnp.cumsum(doc_lengths).astype(jnp.int32)
    blocks = jnp.arange(64, dtype=jnp.int32) * HALF

    def start_of(position):
        return jnp.max(jnp.where(ends[None, :] <= position[:, None], ends[None, :], 0), axis=1)

    lo, hi = start_of(blocks), start_of(blocks + HALF - 1)

    halves_k = keys.reshape(2, HALF, 2, 128)
    halves_v = values.reshape(2, HALF, 2, 128)
    packed = jnp.concatenate([halves_k, halves_v], axis=3)
    pieces = jnp.transpose(packed, (2, 0, 1, 3)).reshape(4, HALF, 256)
    got = jnp.stack([send(pick(pieces, z ^ k), TO_HEAD[k]) for k in range(4)])
    a0 = jnp.stack([pick(got, mine_d ^ plane) for plane in range(4)])

    q_pieces = jnp.transpose(queries.reshape(512, 4, 256), (1, 0, 2))
    q_got = jnp.stack([send(pick(q_pieces, z ^ k), TO_HEAD[k]) for k in range(4)])
    q = jnp.concatenate([pick(q_got, mine_d ^ plane) for plane in range(4)], axis=0)

    a1 = send(a0, X_DOWN)
    a3 = send(a0, X_UP)
    b0 = send(a0, Y_LO)
    near = jnp.stack([a0, a1, a3, b0])
    near_other = send(near, CORE)
    b1 = send(b0, X_DOWN)
    b3 = send(b0, X_UP)
    low = send(jnp.concatenate([a1[:2], b1[:2]], axis=0), X_DOWN)
    high = send(jnp.concatenate([a3[2:], b3[2:]], axis=0), X_UP)
    far = jnp.stack(
        [b1, b3, jnp.concatenate([low[:2], high[:2]], axis=0), jnp.concatenate([low[2:], high[2:]], axis=0)]
    )
    far_other = send(far, CORE)

    here, there = y_lo * 4, (1 - y_lo) * 4
    near_info = jnp.stack([here + x, here + (x + 1) % 4, here + (x + 3) % 4, there + x, j, core]).astype(jnp.int32)
    far_info = jnp.stack(
        [there + (x + 1) % 4, there + (x + 3) % 4, here + (x + 2) % 4, there + (x + 2) % 4, j, core]
    ).astype(jnp.int32)
    state = attention(True, False, near_info, ends, lo, hi, q, near, near_other, ())
    out = attention(False, True, far_info, ends, lo, hi, q, far, far_other, state)

    planes = out.reshape(4, 512, 256)
    back = jnp.stack([send(pick(planes, mine_d ^ k), TO_HOME[k]) for k in range(4)])
    attended = jnp.concatenate([pick(back, z ^ d) for d in range(4)], axis=1)

    by_half = attended.reshape(2, 256, 1024)

    def project(which):
        part = jnp.dot(pick(by_half, which), out_weight, preferred_element_type=jnp.float32).astype(jnp.bfloat16)
        part = part.reshape(2, 128, 4096)
        arrived = send(pick(part, 1 - core), CORE)
        return pick(part, core).astype(jnp.float32) + arrived.astype(jnp.float32)

    far_sum = send(project(1 - y_hi).astype(jnp.bfloat16), Y_HI)
    return (project(y_hi) + far_sum.astype(jnp.float32)).astype(jnp.bfloat16)


def solution(mesh):
    return jax.shard_map(
        on_device,
        mesh=mesh,
        in_specs=(P("ctx", "kv"), P("ctx", "kv"), P("ctx", "kv"), P(), P("kv", None)),
        out_specs=P(("ctx", "kv"), None),
        check_vma=False,
    )
```

```python
import functools
import math

import jax
import jax.numpy as jnp
from jax import lax
from jax.experimental import pallas as pl
from jax.experimental.pallas import tpu as pltpu
from jax.sharding import PartitionSpec as P

HEAD_WIDTH = 128
NEG = -1e30
AXES = ("ctx", "kv")
SCALE2 = HEAD_WIDTH ** -0.5 * math.log2(math.e)
HALF = 256
ROWS = 512
SAFE = 60.0 * math.log2(math.e)


def device_at(z, y_hi, y_lo, x, c):
    return ((z % 4) * 8 + y_lo * 4 + x % 4) * 4 + y_hi * 2 + c


def permutation(move):
    pairs = []
    for i in range(128):
        ctx, kv = divmod(i, 4)
        pairs.append((i, device_at(*move(ctx // 8, kv // 2, ctx // 4 % 2, ctx % 4, kv % 2))))
    return pairs


X_UP = permutation(lambda z, yh, yl, x, c: (z, yh, yl, x + 1, c))
X_TWO = permutation(lambda z, yh, yl, x, c: (z, yh, yl, x + 2, c))
X_DOWN = permutation(lambda z, yh, yl, x, c: (z, yh, yl, x + 3, c))
Y_LO = permutation(lambda z, yh, yl, x, c: (z, yh, 1 - yl, x, c))
Y_HI = permutation(lambda z, yh, yl, x, c: (z, 1 - yh, yl, x, c))
CORE = permutation(lambda z, yh, yl, x, c: (z, yh, yl, x, 1 - c))
TO_HEAD = [
    permutation(lambda z, yh, yl, x, c, k=k: (2 * c + (z ^ k) // 2, yh, yl, x, (z ^ k) % 2))
    for k in range(4)
]
TO_HOME = [[(b, a) for a, b in pairs] for pairs in TO_HEAD]


def send(x, pairs):
    return lax.ppermute(x, AXES, pairs)


def dot_nt(a, b):
    return lax.dot_general(a, b, (((1,), (1,)), ((), ())), preferred_element_type=jnp.float32)


def attention_kernel(first, last, info_ref, ends_ref, lo_ref, hi_ref, q_ref, mine_ref, other_ref, *refs):
    if first:
        flag_in = acc_in = m_in = l_in = None
    else:
        flag_in, acc_in, m_in, l_in = refs[:4]
        refs = refs[4:]
    if last:
        out_ref, acc, m_s, l_s, start_s = refs
    else:
        flag_out, acc_out, m_out, l_out, acc, m_s, l_s, start_s = refs
    own_j = info_ref[4]
    core = info_ref[5]
    ones = jnp.ones((128, 128), jnp.bfloat16)

    def top_square(block):
        return jnp.max(jnp.dot(block * block, ones, preferred_element_type=jnp.float32), axis=0, keepdims=True)

    def k_top(i, top):
        a = top_square(mine_ref[i, :, :, :128].reshape(1024, 128))
        b = top_square(other_ref[i, :, :, :128].reshape(1024, 128))
        return jnp.maximum(top, jnp.maximum(a, b))

    def q_top(i, top):
        rows = pl.ds(pl.multiple_of(i * ROWS, ROWS), ROWS)
        return jnp.maximum(top, jnp.maximum(top_square(q_ref[rows, :128]), top_square(q_ref[rows, 128:])))

    zero = jnp.zeros((1, 128), jnp.float32)
    bound = lax.fori_loop(0, 4, k_top, zero) * lax.fori_loop(0, 4, q_top, zero)
    safe = jnp.max(bound) * 1.02 * SCALE2 * SCALE2 <= SAFE * SAFE
    if not first:
        safe = safe & (flag_in[0] == 1)
    if not last:
        flag_out[0] = jnp.where(safe, 1, 0)

    def q_block(qb, carry):
        gq = (qb * 8 + own_j) * 2
        g_last = gq + 1
        rows = pl.ds(pl.multiple_of(qb * ROWS, ROWS), ROWS)
        lo = lo_ref[gq]
        hi = hi_ref[g_last]

        @pl.when(lo == hi)
        def _():
            start_s[...] = jnp.full_like(start_s, lo)

        @pl.when(lo != hi)
        def _():
            q_pos = gq * 256 + lax.broadcasted_iota(jnp.int32, (ROWS, 128), 0)
            start = jnp.zeros((ROWS, 128), jnp.int32)
            for doc in range(16):
                end = ends_ref[doc]
                start = jnp.maximum(start, jnp.where(q_pos >= end, end, 0))
            start_s[...] = start

        if first:
            acc[...] = jnp.zeros_like(acc)
            m_s[...] = jnp.full_like(m_s, NEG)
            l_s[...] = jnp.zeros_like(l_s)
        else:
            acc[...] = acc_in[rows, :]
            m_s[...] = m_in[rows, :]
            l_s[...] = l_in[rows, :]
        def keys_values(slot, zk):
            k_all = jnp.concatenate([mine_ref[slot, zk, :, :128], other_ref[slot, zk, :, :128]], axis=0)
            v_all = jnp.concatenate([mine_ref[slot, zk, :, 128:], other_ref[slot, zk, :, 128:]], axis=0)
            return k_all, v_all

        def mask_of(gk):
            column = lax.broadcasted_iota(jnp.int32, (ROWS, 512), 1)
            k_pos = gk * 512 + jnp.where(core == 0, column, column ^ 256)
            q_at = gq * 256 + lax.broadcasted_iota(jnp.int32, (ROWS, 512), 0)
            return (k_pos <= q_at) & (k_pos >= start_s[:, :1])

        def quick(slot, zk, gk, masked):
            k_all, v_all = keys_values(slot, zk)
            if masked:
                allowed = mask_of(gk)
            for h in range(2):
                cols = slice(h * 128, (h + 1) * 128)
                p = jnp.exp2(dot_nt(q_ref[rows, cols], k_all) * SCALE2)
                if masked:
                    p = jnp.where(allowed, p, 0.0)
                l_s[:, cols] += (p[:, :128] + p[:, 128:256]) + (p[:, 256:384] + p[:, 384:])
                acc[:, cols] += jnp.dot(p.astype(jnp.bfloat16), v_all, preferred_element_type=jnp.float32)

        def careful(slot, zk, gk):
            k_all, v_all = keys_values(slot, zk)
            allowed = mask_of(gk)
            for h in range(2):
                cols = slice(h * 128, (h + 1) * 128)
                s = jnp.where(allowed, dot_nt(q_ref[rows, cols], k_all), NEG)
                m_old = m_s[:, cols]
                m_new = jnp.maximum(m_old, jnp.max(s, axis=1, keepdims=True))
                shrink = jnp.exp2((m_old - m_new) * SCALE2)
                p = jnp.where(allowed, jnp.exp2((s - m_new[:, :1]) * SCALE2), 0.0)
                m_s[:, cols] = m_new
                l_s[:, cols] = l_s[:, cols] * shrink + (p[:, :128] + p[:, 128:256]) + (p[:, 256:384] + p[:, 384:])
                acc[:, cols] = acc[:, cols] * shrink + jnp.dot(p.astype(jnp.bfloat16), v_all, preferred_element_type=jnp.float32)

        def classify(kb):
            slot = kb // 4
            zk = kb % 4
            gk = zk * 8 + info_ref[slot]
            needed = (gk * 512 <= g_last * 256 + 255) & (gk * 512 + 511 >= lo)
            full = (gk * 512 + 511 <= gq * 256) & (gk * 512 >= hi)
            return slot, zk, gk, needed, full

        def quick2(sa, za, sb, zb):
            ka, va = keys_values(sa, za)
            kb_, vb = keys_values(sb, zb)
            ss = []
            for h in range(2):
                cols = slice(h * 128, (h + 1) * 128)
                ss.append((dot_nt(q_ref[rows, cols], ka), dot_nt(q_ref[rows, cols], kb_)))
            for h in range(2):
                cols = slice(h * 128, (h + 1) * 128)
                pa = jnp.exp2(ss[h][0] * SCALE2)
                pb = jnp.exp2(ss[h][1] * SCALE2)
                l_s[:, cols] += ((pa[:, :128] + pa[:, 128:256]) + (pa[:, 256:384] + pa[:, 384:])) + ((pb[:, :128] + pb[:, 128:256]) + (pb[:, 256:384] + pb[:, 384:]))
                acc[:, cols] += jnp.dot(pa.astype(jnp.bfloat16), va, preferred_element_type=jnp.float32) + jnp.dot(pb.astype(jnp.bfloat16), vb, preferred_element_type=jnp.float32)

        def one(slot, zk, gk, needed, full):
            @pl.when(full & safe)
            def _():
                quick(slot, zk, gk, False)

            @pl.when(needed & jnp.logical_not(full) & safe)
            def _():
                quick(slot, zk, gk, True)

            @pl.when(needed & jnp.logical_not(safe))
            def _():
                careful(slot, zk, gk)

        def k_block(kp, carry):
            a = classify(kp)
            b = classify(kp + 4)
            both = a[4] & b[4] & safe

            @pl.when(both)
            def _():
                quick2(a[0], a[1], b[0], b[1])

            @pl.when(jnp.logical_not(both) & a[3])
            def _():
                one(*a)

            @pl.when(jnp.logical_not(both) & b[3])
            def _():
                one(*b)

            return carry

        def k_pair(i, carry):
            return k_block(i // 4 * 8 + i % 4, carry)

        lax.fori_loop(0, 8, k_pair, 0)
        if last:
            for h in range(2):
                cols = slice(h * 128, (h + 1) * 128)
                total = jnp.sum(l_s[:, cols], axis=1, keepdims=True)
                out_ref[rows, cols] = (acc[:, cols] / total).astype(jnp.bfloat16)
        else:
            acc_out[rows, :] = acc[...]
            l_out[rows, :] = l_s[...]
            for h in range(2):
                cols = slice(h * 128, (h + 1) * 128)
                total = jnp.sum(l_s[:, cols], axis=1, keepdims=True)
                m_out[rows, cols] = jnp.where(safe & (total > 0.0), 0.0, m_s[:, cols])
        return carry

    lax.fori_loop(0, 4, q_block, 0)


def attention(first, last, info, ends, lo, hi, q, mine, other, state):
    rows = q.shape[0]
    whole = pl.BlockSpec(memory_space=pltpu.VMEM)
    scalar = pl.BlockSpec(memory_space=pltpu.SMEM)
    wide = jax.ShapeDtypeStruct((rows, 256), jnp.float32)
    flag = jax.ShapeDtypeStruct((1,), jnp.int32)
    return pl.pallas_call(
        functools.partial(attention_kernel, first, last),
        out_shape=jax.ShapeDtypeStruct((rows, 256), jnp.bfloat16) if last else (flag, wide, wide, wide),
        in_specs=[scalar] * 4 + [whole] * 3 + ([] if first else [scalar] + [whole] * 3),
        out_specs=whole if last else (scalar, whole, whole, whole),
        scratch_shapes=[pltpu.VMEM((ROWS, 256), jnp.float32)] * 3 + [pltpu.VMEM((ROWS, 128), jnp.int32)],
        compiler_params=pltpu.CompilerParams(vmem_limit_bytes=40 * 1024 * 1024),
        cost_estimate=pl.CostEstimate(
            flops=12_000_000_000, bytes_accessed=8 * 1024 * 1024, transcendentals=12_000_000
        ),
        name="attend_last" if last else "attend_first",
    )(info, ends, lo, hi, q, mine, other, *state)


def pick(stacked, index):
    return lax.dynamic_index_in_dim(stacked, index, 0, keepdims=False)


def on_device(queries, keys, values, doc_lengths, out_weight):
    ctx = lax.axis_index("ctx")
    kv = lax.axis_index("kv")
    z, y_lo, x = ctx // 8, ctx // 4 % 2, ctx % 4
    y_hi, core = kv // 2, kv % 2
    j = ctx % 8
    mine_d = 2 * (z % 2) + core
    ends = jnp.cumsum(doc_lengths).astype(jnp.int32)
    blocks = jnp.arange(64, dtype=jnp.int32) * HALF

    def start_of(position):
        return jnp.max(jnp.where(ends[None, :] <= position[:, None], ends[None, :], 0), axis=1)

    lo, hi = start_of(blocks), start_of(blocks + HALF - 1)

    def kv_piece(d):
        at = (d % 2 * HALF, d // 2 * 128)
        return jnp.concatenate(
            [lax.dynamic_slice(keys, at, (HALF, 128)), lax.dynamic_slice(values, at, (HALF, 128))], axis=1
        )

    got = jnp.stack([send(kv_piece(z ^ k), TO_HEAD[k]) for k in range(4)])
    a0 = jnp.stack([pick(got, mine_d ^ plane) for plane in range(4)])

    a0, queries = lax.optimization_barrier((a0, queries))
    q_got = jnp.stack(
        [send(lax.dynamic_slice(queries, (0, (z ^ k) * 256), (512, 256)), TO_HEAD[k]) for k in range(4)]
    )
    q = jnp.concatenate([pick(q_got, mine_d ^ plane) for plane in range(4)], axis=0)

    b0 = send(a0, Y_LO)
    a1 = send(a0, X_DOWN)
    a3 = send(a0, X_UP)
    b0, a1, a3, q = lax.optimization_barrier((b0, a1, a3, q))
    near = jnp.stack([a0, a1, a3, b0])
    near_other = send(near, CORE)
    a2 = send(a1, X_DOWN)
    b3 = send(b0, X_UP)
    b1 = send(a1, Y_LO)
    b2 = send(b0, X_TWO)
    here, there = y_lo * 4, (1 - y_lo) * 4
    near_info = jnp.stack([here + x, here + (x + 1) % 4, here + (x + 3) % 4, there + x, j, core]).astype(jnp.int32)
    far_info = jnp.stack(
        [there + (x + 1) % 4, there + (x + 3) % 4, here + (x + 2) % 4, there + (x + 2) % 4, j, core]
    ).astype(jnp.int32)
    state = attention(True, False, near_info, ends, lo, hi, q, near, near_other, ())
    b1, b3, a2, b2, state = lax.optimization_barrier((b1, b3, a2, b2, state))
    far = jnp.stack([b1, b3, a2, b2])
    far_other = send(far, CORE)
    out = attention(False, True, far_info, ends, lo, hi, q, far, far_other, state)

    planes = out.reshape(4, 512, 256)
    back = jnp.stack([send(pick(planes, mine_d ^ k), TO_HOME[k]) for k in range(4)])
    attended = jnp.concatenate([pick(back, z ^ d) for d in range(4)], axis=1)

    by_half = attended.reshape(2, 256, 1024)

    def project(which):
        part = jnp.dot(pick(by_half, which), out_weight, preferred_element_type=jnp.float32).astype(jnp.bfloat16)
        part = part.reshape(2, 128, 4096)
        arrived = send(pick(part, 1 - core), CORE)
        return pick(part, core).astype(jnp.float32) + arrived.astype(jnp.float32)

    far_sum = send(project(1 - y_hi).astype(jnp.bfloat16), Y_HI)
    return (project(y_hi) + far_sum.astype(jnp.float32)).astype(jnp.bfloat16)


def solution(mesh):
    return jax.shard_map(
        on_device,
        mesh=mesh,
        in_specs=(P("ctx", "kv"), P("ctx", "kv"), P("ctx", "kv"), P(), P("kv", None)),
        out_specs=P(("ctx", "kv"), None),
        check_vma=False,
    )
```

```python
import functools
import math

import jax
import jax.numpy as jnp
from jax import lax
from jax.experimental import pallas as pl
from jax.experimental.pallas import tpu as pltpu
from jax.sharding import PartitionSpec as P

HEAD_WIDTH = 128
NEG = -1e30
AXES = ("ctx", "kv")
SCALE2 = HEAD_WIDTH ** -0.5 * math.log2(math.e)
HALF = 256
ROWS = 512
SAFE = 60.0 * math.log2(math.e)


def device_at(z, y_hi, y_lo, x, c):
    return ((z % 4) * 8 + y_lo * 4 + x % 4) * 4 + y_hi * 2 + c


def permutation(move):
    pairs = []
    for i in range(128):
        ctx, kv = divmod(i, 4)
        pairs.append((i, device_at(*move(ctx // 8, kv // 2, ctx // 4 % 2, ctx % 4, kv % 2))))
    return pairs


X_UP = permutation(lambda z, yh, yl, x, c: (z, yh, yl, x + 1, c))
X_TWO = permutation(lambda z, yh, yl, x, c: (z, yh, yl, x + 2, c))
X_DOWN = permutation(lambda z, yh, yl, x, c: (z, yh, yl, x + 3, c))
Y_LO = permutation(lambda z, yh, yl, x, c: (z, yh, 1 - yl, x, c))
Y_HI = permutation(lambda z, yh, yl, x, c: (z, 1 - yh, yl, x, c))
CORE = permutation(lambda z, yh, yl, x, c: (z, yh, yl, x, 1 - c))
TO_HEAD = [
    permutation(lambda z, yh, yl, x, c, k=k: (2 * c + (z ^ k) // 2, yh, yl, x, (z ^ k) % 2))
    for k in range(4)
]
TO_HOME = [[(b, a) for a, b in pairs] for pairs in TO_HEAD]


def send(x, pairs):
    return lax.ppermute(x, AXES, pairs)


def dot_nt(a, b):
    return lax.dot_general(a, b, (((1,), (1,)), ((), ())), preferred_element_type=jnp.float32)


def fold(p):
    total = p[:, :128]
    for at in range(128, p.shape[1], 128):
        total += p[:, at : at + 128]
    return total


def no_reference_needed(q_ref, mine_ref, other_ref):
    ones = jnp.ones((128, 128), jnp.bfloat16)

    def top_square(block):
        return jnp.max(jnp.dot(block * block, ones, preferred_element_type=jnp.float32), axis=0, keepdims=True)

    def k_top(i, top):
        a = top_square(mine_ref[i, :, :, :128].reshape(1024, 128))
        b = top_square(other_ref[i, :, :, :128].reshape(1024, 128))
        return jnp.maximum(top, jnp.maximum(a, b))

    def q_top(i, top):
        rows = pl.ds(pl.multiple_of(i * ROWS, ROWS), ROWS)
        return jnp.maximum(top, jnp.maximum(top_square(q_ref[rows, :128]), top_square(q_ref[rows, 128:])))

    zero = jnp.zeros((1, 128), jnp.float32)
    bound = lax.fori_loop(0, 4, k_top, zero) * lax.fori_loop(0, 4, q_top, zero)
    return jnp.max(bound) * 1.02 * SCALE2 * SCALE2 <= SAFE * SAFE


def attend_blocks(tile, first_pos, info_ref, ends_ref, lo, hi, safe, mine_ref, other_ref, q_s, acc, m_s, l_s, start_s):
    core = info_ref[5]

    @pl.when(lo == hi)
    def _():
        start_s[...] = jnp.full_like(start_s, lo)

    @pl.when(lo != hi)
    def _():
        q_pos = first_pos + lax.broadcasted_iota(jnp.int32, (tile, 128), 0)
        start = jnp.zeros((tile, 128), jnp.int32)
        for doc in range(16):
            end = ends_ref[doc]
            start = jnp.maximum(start, jnp.where(q_pos >= end, end, 0))
        start_s[...] = start

    def keys_values(slot, zk):
        k_all = jnp.concatenate([mine_ref[slot, zk, :, :128], other_ref[slot, zk, :, :128]], axis=0)
        v_all = jnp.concatenate([mine_ref[slot, zk, :, 128:], other_ref[slot, zk, :, 128:]], axis=0)
        return k_all, v_all

    def mask_of(gk):
        column = lax.broadcasted_iota(jnp.int32, (tile, 512), 1)
        k_pos = gk * 512 + jnp.where(core == 0, column, column ^ 256)
        q_at = first_pos + lax.broadcasted_iota(jnp.int32, (tile, 512), 0)
        return (k_pos <= q_at) & (k_pos >= start_s[:, :1])

    parts = [slice(0, tile), slice(tile, 2 * tile)] if tile == ROWS else [slice(0, 2 * tile)]

    def quick(slot, zk, gk, masked):
        k_all, v_all = keys_values(slot, zk)
        if masked:
            allowed = mask_of(gk)
            if tile < ROWS:
                allowed = jnp.concatenate([allowed, allowed], axis=0)
        for part in parts:
            p = jnp.exp2(dot_nt(q_s[part, :], k_all) * SCALE2)
            if masked:
                p = jnp.where(allowed, p, 0.0)
            l_s[part, :] += fold(p)
            acc[part, :] += jnp.dot(p.astype(jnp.bfloat16), v_all, preferred_element_type=jnp.float32)

    def quick_two(slot_a, zk_a, slot_b, zk_b):
        k_a, v_a = keys_values(slot_a, zk_a)
        k_b, v_b = keys_values(slot_b, zk_b)
        scores = [(dot_nt(q_s[part, :], k_a), dot_nt(q_s[part, :], k_b)) for part in parts]
        for part, (s_a, s_b) in zip(parts, scores):
            p_a = jnp.exp2(s_a * SCALE2)
            p_b = jnp.exp2(s_b * SCALE2)
            l_s[part, :] += fold(p_a) + fold(p_b)
            acc[part, :] += jnp.dot(
                p_a.astype(jnp.bfloat16), v_a, preferred_element_type=jnp.float32
            ) + jnp.dot(p_b.astype(jnp.bfloat16), v_b, preferred_element_type=jnp.float32)

    def careful(slot, zk, gk):
        k_all, v_all = keys_values(slot, zk)
        allowed = mask_of(gk)
        for h in range(2):
            part = slice(h * tile, (h + 1) * tile)
            s = jnp.where(allowed, dot_nt(q_s[part, :], k_all), NEG)
            m_old = m_s[part, :]
            m_new = jnp.maximum(m_old, jnp.max(s, axis=1, keepdims=True))
            shrink = jnp.exp2((m_old - m_new) * SCALE2)
            p = jnp.where(allowed, jnp.exp2((s - m_new[:, :1]) * SCALE2), 0.0)
            m_s[part, :] = m_new
            l_s[part, :] = l_s[part, :] * shrink + fold(p)
            acc[part, :] = acc[part, :] * shrink + jnp.dot(
                p.astype(jnp.bfloat16), v_all, preferred_element_type=jnp.float32
            )

    def classify(kb):
        slot = kb // 4
        zk = kb % 4
        gk = zk * 8 + info_ref[slot]
        needed = (gk * 512 <= first_pos + tile - 1) & (gk * 512 + 511 >= lo)
        full = (gk * 512 + 511 <= first_pos) & (gk * 512 >= hi)
        return slot, zk, gk, needed, full

    def one(slot, zk, gk, needed, full):
        @pl.when(full & safe)
        def _():
            quick(slot, zk, gk, False)

        @pl.when(needed & jnp.logical_not(full) & safe)
        def _():
            quick(slot, zk, gk, True)

        @pl.when(needed & jnp.logical_not(safe))
        def _():
            careful(slot, zk, gk)

    def k_pair(i, carry):
        kb = i // 4 * 8 + i % 4
        a, b = classify(kb), classify(kb + 4)
        both = a[4] & b[4] & safe

        @pl.when(both)
        def _():
            quick_two(a[0], a[1], b[0], b[1])

        @pl.when(jnp.logical_not(both) & (a[3] | b[3]))
        def _():
            one(*a)
            one(*b)

        return carry

    lax.fori_loop(0, 8, k_pair, 0)


def near_kernel(info_ref, ends_ref, lo_ref, hi_ref, q_ref, mine_ref, other_ref, flag_ref, *refs):
    outs, (q_s, acc, m_s, l_s, start_s) = refs[:4], refs[4:]
    safe = no_reference_needed(q_ref, mine_ref, other_ref)
    flag_ref[0] = jnp.where(safe, 1, 0)
    ahead = info_ref[6]

    def q_block(plane, carry):
        gq = (plane * 8 + info_ref[4]) * 2
        rows = pl.ds(pl.multiple_of(plane * ROWS, ROWS), ROWS)
        for h in range(2):
            q_s[h * ROWS : (h + 1) * ROWS, :] = q_ref[rows, h * 128 : (h + 1) * 128]
        acc[...] = jnp.zeros_like(acc)
        m_s[...] = jnp.full_like(m_s, NEG)
        l_s[...] = jnp.zeros_like(l_s)
        attend_blocks(
            ROWS, gq * HALF, info_ref, ends_ref, lo_ref[gq], hi_ref[gq + 1], safe,
            mine_ref, other_ref, q_s, acc, m_s, l_s, start_s,
        )

        @pl.when(jnp.logical_not(safe))
        def _():
            lane = lax.broadcasted_iota(jnp.int32, l_s.shape, 1)
            l_s[...] = jnp.where(lane < 64, jnp.sum(l_s[...], axis=1, keepdims=True), m_s[...])

        at = pl.ds(pl.multiple_of(plane * HALF, HALF), HALF)
        for part, half in ((0, ahead), (1, 1 - ahead)):
            for h in range(2):
                rows_s = pl.ds(pl.multiple_of(h * ROWS + half * HALF, HALF), HALF)
                outs[part][at, h * 128 : (h + 1) * 128] = acc[rows_s, :]
                outs[2 + part][at, h * 128 : (h + 1) * 128] = l_s[rows_s, :]
        return carry

    lax.fori_loop(0, 4, q_block, 0)


def far_kernel(ahead, info_ref, ends_ref, lo_ref, hi_ref, flag_in, q_ref, mine_ref, other_ref, acc_in, l_in, *refs):
    near_safe = flag_in[0] == 1
    if ahead:
        out_ref, flag_ref, q_s, acc, m_s, l_s, start_s = refs
        safe = near_safe & no_reference_needed(q_ref, mine_ref, other_ref)
        flag_ref[0] = jnp.where(near_safe, 1, 0)
        flag_ref[1] = jnp.where(safe, 1, 0)
        half = info_ref[6]
    else:
        out_ref, q_s, acc, m_s, l_s, start_s = refs
        safe = flag_in[1] == 1
        half = 1 - info_ref[6]

    def q_block(plane, carry):
        gq = (plane * 8 + info_ref[4]) * 2 + half
        rows = pl.ds(pl.multiple_of(plane * ROWS + half * HALF, HALF), HALF)
        at = pl.ds(pl.multiple_of(plane * HALF, HALF), HALF)
        for h in range(2):
            part, cols = slice(h * HALF, (h + 1) * HALF), slice(h * 128, (h + 1) * 128)
            q_s[part, :] = q_ref[rows, cols]
            acc[part, :] = acc_in[at, cols]
            l_s[part, :] = l_in[at, cols]

        @pl.when(jnp.logical_not(safe))
        def _():
            lane = lax.broadcasted_iota(jnp.int32, l_s.shape, 1)
            old = l_s[...]
            total = jnp.sum(old, axis=1, keepdims=True)
            row_sum = jnp.where(near_safe, total, old[:, :1])
            reference = jnp.where(near_safe, jnp.where(total > 0.0, 0.0, NEG), old[:, 64:65])
            l_s[...] = jnp.where(lane == 0, row_sum, 0.0)
            m_s[...] = jnp.broadcast_to(reference, m_s.shape)

        attend_blocks(
            HALF, gq * HALF, info_ref, ends_ref, lo_ref[gq], hi_ref[gq], safe,
            mine_ref, other_ref, q_s, acc, m_s, l_s, start_s,
        )
        for h in range(2):
            part, cols = slice(h * HALF, (h + 1) * HALF), slice(h * 128, (h + 1) * 128)
            total = jnp.sum(l_s[part, :], axis=1, keepdims=True)
            out_ref[at, cols] = (acc[part, :] / total).astype(jnp.bfloat16)
        return carry

    lax.fori_loop(0, 4, q_block, 0)


def kernel_call(kernel, name, share, tile, outs, out_flags, args, scalars):
    whole = pl.BlockSpec(memory_space=pltpu.VMEM)
    scalar = pl.BlockSpec(memory_space=pltpu.SMEM)
    return pl.pallas_call(
        kernel,
        out_shape=outs,
        in_specs=[scalar] * scalars + [whole] * (len(args) - scalars),
        out_specs=tuple(scalar if flag else whole for flag in out_flags),
        scratch_shapes=[pltpu.VMEM((2 * tile, 128), jnp.bfloat16)]
        + [pltpu.VMEM((2 * tile, 128), jnp.float32)] * 3
        + [pltpu.VMEM((tile, 128), jnp.int32)],
        compiler_params=pltpu.CompilerParams(vmem_limit_bytes=40 * 1024 * 1024),
        cost_estimate=pl.CostEstimate(
            flops=12_000_000_000 // share, bytes_accessed=8 * 1024 * 1024, transcendentals=12_000_000 // share
        ),
        name=name,
    )(*args)


def pick(stacked, index):
    return lax.dynamic_index_in_dim(stacked, index, 0, keepdims=False)


def on_device(queries, keys, values, doc_lengths, out_weight):
    ctx = lax.axis_index("ctx")
    kv = lax.axis_index("kv")
    z, y_lo, x = ctx // 8, ctx // 4 % 2, ctx % 4
    y_hi, core = kv // 2, kv % 2
    j = ctx % 8
    mine_d = 2 * (z % 2) + core
    ends = jnp.cumsum(doc_lengths).astype(jnp.int32)
    blocks = jnp.arange(64, dtype=jnp.int32) * HALF

    def start_of(position):
        return jnp.max(jnp.where(ends[None, :] <= position[:, None], ends[None, :], 0), axis=1)

    lo, hi = start_of(blocks), start_of(blocks + HALF - 1)

    def kv_piece(d):
        at = (d % 2 * HALF, d // 2 * 128)
        return jnp.concatenate(
            [lax.dynamic_slice(keys, at, (HALF, 128)), lax.dynamic_slice(values, at, (HALF, 128))], axis=1
        )

    def q_piece(d):
        return lax.dynamic_slice(queries, (0, d * 256), (512, 256))

    got = [send(kv_piece(z ^ k), TO_HEAD[k]) for k in range(4)]
    q_got = [send(q_piece(z ^ k), TO_HEAD[k]) for k in range(2)]
    *got, queries = lax.optimization_barrier(tuple(got) + tuple(q_got) + (queries,))
    got, q_got = got[:4], got[4:]
    got = jnp.stack(got)
    a0 = jnp.stack([pick(got, mine_d ^ plane) for plane in range(4)])

    b0 = send(a0, Y_LO)
    a1 = send(a0, X_DOWN)
    a3 = send(a0, X_UP)
    q_got = jnp.stack(q_got + [send(q_piece(z ^ k), TO_HEAD[k]) for k in range(2, 4)])
    q = jnp.concatenate([pick(q_got, mine_d ^ plane) for plane in range(4)], axis=0)
    b0, a1, a3, q = lax.optimization_barrier((b0, a1, a3, q))
    near = jnp.stack([a0, a1, a3, b0])
    near_other = send(near, CORE)
    a2 = send(a1, X_DOWN)
    b3 = send(b0, X_UP)
    b1 = send(a1, Y_LO)
    b2 = send(b0, X_TWO)
    here, there = y_lo * 4, (1 - y_lo) * 4
    near_info = jnp.stack([here + x, here + (x + 1) % 4, here + (x + 3) % 4, there + x, j, core, 1 - y_hi]).astype(jnp.int32)
    far_info = jnp.stack(
        [there + (x + 1) % 4, there + (x + 3) % 4, here + (x + 2) % 4, there + (x + 2) % 4, j, core, 1 - y_hi]
    ).astype(jnp.int32)
    flag = jax.ShapeDtypeStruct((2,), jnp.int32)
    wide = jax.ShapeDtypeStruct((1024, 256), jnp.float32)
    narrow = jax.ShapeDtypeStruct((1024, 256), jnp.bfloat16)
    state = kernel_call(
        near_kernel, "attend_near", 1, ROWS, (flag, wide, wide, wide, wide), (1, 0, 0, 0, 0),
        (near_info, ends, lo, hi, q, near, near_other), 4,
    )
    b1, b3, a2, b2, *state = lax.optimization_barrier((b1, b3, a2, b2) + tuple(state))
    flags, acc_ahead, acc_own, l_ahead, l_own = state
    far = jnp.stack([b1, b3, a2, b2])
    far_other = send(far, CORE)
    out_ahead, flags = kernel_call(
        functools.partial(far_kernel, True), "attend_ahead", 2, HALF, (narrow, flag), (0, 1),
        (far_info, ends, lo, hi, flags, q, far, far_other, acc_ahead, l_ahead), 5,
    )

    def send_home(out):
        planes = out.reshape(4, 256, 256)
        return tuple(send(pick(planes, mine_d ^ k), TO_HOME[k]) for k in range(4))

    back_ahead = send_home(out_ahead)
    (out_own,) = kernel_call(
        functools.partial(far_kernel, False), "attend_own", 2, HALF, (narrow,), (0,),
        (far_info, ends, lo, hi, flags, q, far, far_other, acc_own, l_own), 5,
    )
    *back_ahead, out_own = lax.optimization_barrier(back_ahead + (out_own,))
    back_own = send_home(out_own)

    def project(back):
        back = jnp.stack(back)
        attended = jnp.concatenate([pick(back, z ^ d) for d in range(4)], axis=1)
        part = jnp.dot(attended, out_weight, preferred_element_type=jnp.float32).astype(jnp.bfloat16)
        part = part.reshape(2, 128, 4096)
        arrived = send(pick(part, 1 - core), CORE)
        return pick(part, core).astype(jnp.float32) + arrived.astype(jnp.float32)

    far_sum = send(project(back_ahead).astype(jnp.bfloat16), Y_HI)
    return (project(back_own) + far_sum.astype(jnp.float32)).astype(jnp.bfloat16)


def solution(mesh):
    return jax.shard_map(
        on_device,
        mesh=mesh,
        in_specs=(P("ctx", "kv"), P("ctx", "kv"), P("ctx", "kv"), P(), P("kv", None)),
        out_specs=P(("ctx", "kv"), None),
        check_vma=False,
    )
```

```python
import functools
import math

import jax
import jax.numpy as jnp
from jax import lax
from jax.experimental import pallas as pl
from jax.experimental.pallas import tpu as pltpu
from jax.sharding import PartitionSpec as P

HEAD_WIDTH = 128
NEG = -1e30
AXES = ("ctx", "kv")
SCALE2 = HEAD_WIDTH ** -0.5 * math.log2(math.e)
HALF = 256
ROWS = 512
SAFE = 60.0 * math.log2(math.e)


def device_at(z, y_hi, y_lo, x, c):
    return ((z % 4) * 8 + y_lo * 4 + x % 4) * 4 + y_hi * 2 + c


def permutation(move):
    pairs = []
    for i in range(128):
        ctx, kv = divmod(i, 4)
        pairs.append((i, device_at(*move(ctx // 8, kv // 2, ctx // 4 % 2, ctx % 4, kv % 2))))
    return pairs


X_UP = permutation(lambda z, yh, yl, x, c: (z, yh, yl, x + 1, c))
X_TWO = permutation(lambda z, yh, yl, x, c: (z, yh, yl, x + 2, c))
X_DOWN = permutation(lambda z, yh, yl, x, c: (z, yh, yl, x + 3, c))
Y_LO = permutation(lambda z, yh, yl, x, c: (z, yh, 1 - yl, x, c))
Y_HI = permutation(lambda z, yh, yl, x, c: (z, 1 - yh, yl, x, c))
CORE = permutation(lambda z, yh, yl, x, c: (z, yh, yl, x, 1 - c))
TO_HEAD = [
    permutation(lambda z, yh, yl, x, c, k=k: (2 * c + (z ^ k) // 2, yh, yl, x, (z ^ k) % 2))
    for k in range(4)
]


def to_home(half_of):
    pairs_of = []
    for pairs in TO_HEAD:
        back = []
        for home, head in pairs:
            ctx, kv = divmod(head, 4)
            back.append(((ctx ^ (4 * half_of(kv // 2))) * 4 + kv, home))
        pairs_of.append(back)
    return pairs_of


AHEAD_HOME = to_home(lambda y_hi: 1 - y_hi)
OWN_HOME = to_home(lambda y_hi: y_hi)


def send(x, pairs):
    return lax.ppermute(x, AXES, pairs)


def dot_nt(a, b):
    return lax.dot_general(a, b, (((1,), (1,)), ((), ())), preferred_element_type=jnp.float32)


def fold(p):
    total = p[:, :128]
    for at in range(128, p.shape[1], 128):
        total += p[:, at : at + 128]
    return total


def no_reference_needed(q_ref, mine_ref, other_ref):
    ones = jnp.ones((128, 128), jnp.bfloat16)

    def top_square(block):
        return jnp.max(jnp.dot(block * block, ones, preferred_element_type=jnp.float32), axis=0, keepdims=True)

    def k_top(i, top):
        a = top_square(mine_ref[i, :, :, :128].reshape(1024, 128))
        b = top_square(other_ref[i, :, :, :128].reshape(1024, 128))
        return jnp.maximum(top, jnp.maximum(a, b))

    def q_top(i, top):
        a = top_square(q_ref[i % 2, pl.ds(i // 2 * 2, 2), :, :128].reshape(512, 128))
        b = top_square(q_ref[i % 2, pl.ds(i // 2 * 2, 2), :, 128:].reshape(512, 128))
        return jnp.maximum(top, jnp.maximum(a, b))

    zero = jnp.zeros((1, 128), jnp.float32)
    bound = lax.fori_loop(0, 4, k_top, zero) * lax.fori_loop(0, 4, q_top, zero)
    return jnp.max(bound) * 1.02 * SCALE2 * SCALE2 <= SAFE * SAFE


def attend_blocks(tile, first_pos, info_ref, ends_ref, lo, hi, safe, mine_ref, other_ref, q_s, acc, m_s, l_s, start_s):
    core = info_ref[5]

    @pl.when(lo == hi)
    def _():
        start_s[...] = jnp.full_like(start_s, lo)

    @pl.when(lo != hi)
    def _():
        q_pos = first_pos + lax.broadcasted_iota(jnp.int32, (tile, 128), 0)
        start = jnp.zeros((tile, 128), jnp.int32)
        for doc in range(16):
            end = ends_ref[doc]
            start = jnp.maximum(start, jnp.where(q_pos >= end, end, 0))
        start_s[...] = start

    def keys_values(slot, zk):
        k_all = jnp.concatenate([mine_ref[slot, zk, :, :128], other_ref[slot, zk, :, :128]], axis=0)
        v_all = jnp.concatenate([mine_ref[slot, zk, :, 128:], other_ref[slot, zk, :, 128:]], axis=0)
        return k_all, v_all

    def mask_of(gk):
        column = lax.broadcasted_iota(jnp.int32, (tile, 512), 1)
        k_pos = gk * 512 + jnp.where(core == 0, column, column ^ 256)
        q_at = first_pos + lax.broadcasted_iota(jnp.int32, (tile, 512), 0)
        return (k_pos <= q_at) & (k_pos >= start_s[:, :1])

    def quick(slot, zk, gk, masked):
        k_all, v_all = keys_values(slot, zk)
        p = jnp.exp2(dot_nt(q_s[...], k_all) * SCALE2)
        if masked:
            allowed = mask_of(gk)
            p = jnp.where(jnp.concatenate([allowed, allowed], axis=0), p, 0.0)
        l_s[...] += fold(p)
        acc[...] += jnp.dot(p.astype(jnp.bfloat16), v_all, preferred_element_type=jnp.float32)

    def quick_two(slot_a, zk_a, slot_b, zk_b):
        k_a, v_a = keys_values(slot_a, zk_a)
        k_b, v_b = keys_values(slot_b, zk_b)
        s_a, s_b = dot_nt(q_s[...], k_a), dot_nt(q_s[...], k_b)
        p_a, p_b = jnp.exp2(s_a * SCALE2), jnp.exp2(s_b * SCALE2)
        l_s[...] += fold(p_a) + fold(p_b)
        acc[...] += jnp.dot(p_a.astype(jnp.bfloat16), v_a, preferred_element_type=jnp.float32) + jnp.dot(
            p_b.astype(jnp.bfloat16), v_b, preferred_element_type=jnp.float32
        )

    def careful(slot, zk, gk):
        k_all, v_all = keys_values(slot, zk)
        allowed = mask_of(gk)
        for h in range(2):
            part = slice(h * tile, (h + 1) * tile)
            s = jnp.where(allowed, dot_nt(q_s[part, :], k_all), NEG)
            m_old = m_s[part, :]
            m_new = jnp.maximum(m_old, jnp.max(s, axis=1, keepdims=True))
            shrink = jnp.exp2((m_old - m_new) * SCALE2)
            p = jnp.where(allowed, jnp.exp2((s - m_new[:, :1]) * SCALE2), 0.0)
            m_s[part, :] = m_new
            l_s[part, :] = l_s[part, :] * shrink + fold(p)
            acc[part, :] = acc[part, :] * shrink + jnp.dot(
                p.astype(jnp.bfloat16), v_all, preferred_element_type=jnp.float32
            )

    def classify(kb):
        slot = kb // 4
        zk = kb % 4
        gk = zk * 8 + info_ref[slot]
        needed = (gk * 512 <= first_pos + tile - 1) & (gk * 512 + 511 >= lo)
        full = (gk * 512 + 511 <= first_pos) & (gk * 512 >= hi)
        return slot, zk, gk, needed, full

    def one(slot, zk, gk, needed, full):
        @pl.when(full & safe)
        def _():
            quick(slot, zk, gk, False)

        @pl.when(needed & jnp.logical_not(full) & safe)
        def _():
            quick(slot, zk, gk, True)

        @pl.when(needed & jnp.logical_not(safe))
        def _():
            careful(slot, zk, gk)

    def k_pair(i, carry):
        kb = i // 4 * 8 + i % 4
        a, b = classify(kb), classify(kb + 4)
        both = a[4] & b[4] & safe

        @pl.when(both)
        def _():
            quick_two(a[0], a[1], b[0], b[1])

        @pl.when(jnp.logical_not(both) & (a[3] | b[3]))
        def _():
            one(*a)
            one(*b)

        return carry

    lax.fori_loop(0, 8, k_pair, 0)


def near_kernel(info_ref, ends_ref, lo_ref, hi_ref, q_ref, mine_ref, other_ref, flag_ref, *refs):
    outs, (q_s, acc, m_s, l_s, start_s) = refs[:4], refs[4:]
    safe = no_reference_needed(q_ref, mine_ref, other_ref)
    flag_ref[0] = jnp.where(safe, 1, 0)
    ahead = info_ref[6]

    def q_block(i, carry):
        half, plane = i // 4, i % 4
        gq = (plane * 8 + (info_ref[4] ^ (4 * half))) * 2 + half
        for h in range(2):
            q_s[h * HALF : (h + 1) * HALF, :] = q_ref[half, plane, :, h * 128 : (h + 1) * 128]
        acc[...] = jnp.zeros_like(acc)
        m_s[...] = jnp.full_like(m_s, NEG)
        l_s[...] = jnp.zeros_like(l_s)
        attend_blocks(
            HALF, gq * HALF, info_ref, ends_ref, lo_ref[gq], hi_ref[gq], safe,
            mine_ref, other_ref, q_s, acc, m_s, l_s, start_s,
        )

        @pl.when(jnp.logical_not(safe))
        def _():
            lane = lax.broadcasted_iota(jnp.int32, l_s.shape, 1)
            l_s[...] = jnp.where(lane < 64, jnp.sum(l_s[...], axis=1, keepdims=True), m_s[...])

        def store(part):
            outs[part][plane] = acc[...]
            outs[2 + part][plane] = l_s[...]

        @pl.when(half == ahead)
        def _():
            store(0)

        @pl.when(half != ahead)
        def _():
            store(1)

        return carry

    lax.fori_loop(0, 8, q_block, 0)


def far_kernel(ahead, info_ref, ends_ref, lo_ref, hi_ref, flag_in, q_ref, mine_ref, other_ref, acc_in, l_in, *refs):
    near_safe = flag_in[0] == 1
    if ahead:
        out_ref, flag_ref, q_s, acc, m_s, l_s, start_s = refs
        safe = near_safe & no_reference_needed(q_ref, mine_ref, other_ref)
        flag_ref[0] = jnp.where(near_safe, 1, 0)
        flag_ref[1] = jnp.where(safe, 1, 0)
        half = info_ref[6]
    else:
        out_ref, q_s, acc, m_s, l_s, start_s = refs
        safe = flag_in[1] == 1
        half = 1 - info_ref[6]

    def q_block(plane, carry):
        gq = (plane * 8 + (info_ref[4] ^ (4 * half))) * 2 + half
        for h in range(2):
            q_s[h * HALF : (h + 1) * HALF, :] = q_ref[half, plane, :, h * 128 : (h + 1) * 128]
        acc[...] = acc_in[plane]
        l_s[...] = l_in[plane]

        @pl.when(jnp.logical_not(safe))
        def _():
            lane = lax.broadcasted_iota(jnp.int32, l_s.shape, 1)
            old = l_s[...]
            total = jnp.sum(old, axis=1, keepdims=True)
            row_sum = jnp.where(near_safe, total, old[:, :1])
            reference = jnp.where(near_safe, jnp.where(total > 0.0, 0.0, NEG), old[:, 64:65])
            l_s[...] = jnp.where(lane == 0, row_sum, 0.0)
            m_s[...] = jnp.broadcast_to(reference, m_s.shape)

        attend_blocks(
            HALF, gq * HALF, info_ref, ends_ref, lo_ref[gq], hi_ref[gq], safe,
            mine_ref, other_ref, q_s, acc, m_s, l_s, start_s,
        )
        for h in range(2):
            part, cols = slice(h * HALF, (h + 1) * HALF), slice(h * 128, (h + 1) * 128)
            total = jnp.sum(l_s[part, :], axis=1, keepdims=True)
            out_ref[plane, :, cols] = (acc[part, :] / total).astype(jnp.bfloat16)
        return carry

    lax.fori_loop(0, 4, q_block, 0)


def kernel_call(kernel, name, share, tile, outs, out_flags, args, scalars):
    whole = pl.BlockSpec(memory_space=pltpu.VMEM)
    scalar = pl.BlockSpec(memory_space=pltpu.SMEM)
    return pl.pallas_call(
        kernel,
        out_shape=outs,
        in_specs=[scalar] * scalars + [whole] * (len(args) - scalars),
        out_specs=tuple(scalar if flag else whole for flag in out_flags),
        scratch_shapes=[pltpu.VMEM((2 * tile, 128), jnp.bfloat16)]
        + [pltpu.VMEM((2 * tile, 128), jnp.float32)] * 3
        + [pltpu.VMEM((tile, 128), jnp.int32)],
        compiler_params=pltpu.CompilerParams(vmem_limit_bytes=40 * 1024 * 1024),
        cost_estimate=pl.CostEstimate(
            flops=12_000_000_000 // share, bytes_accessed=8 * 1024 * 1024, transcendentals=12_000_000 // share
        ),
        name=name,
    )(*args)


def pick(stacked, index):
    return lax.dynamic_index_in_dim(stacked, index, 0, keepdims=False)


def on_device(queries, keys, values, doc_lengths, out_weight):
    ctx = lax.axis_index("ctx")
    kv = lax.axis_index("kv")
    z, y_lo, x = ctx // 8, ctx // 4 % 2, ctx % 4
    y_hi, core = kv // 2, kv % 2
    j = ctx % 8
    mine_d = 2 * (z % 2) + core
    ends = jnp.cumsum(doc_lengths).astype(jnp.int32)
    blocks = jnp.arange(64, dtype=jnp.int32) * HALF

    def start_of(position):
        return jnp.max(jnp.where(ends[None, :] <= position[:, None], ends[None, :], 0), axis=1)

    lo, hi = start_of(blocks), start_of(blocks + HALF - 1)

    def kv_piece(d):
        at = (d % 2 * HALF, d // 2 * 128)
        return jnp.concatenate(
            [lax.dynamic_slice(keys, at, (HALF, 128)), lax.dynamic_slice(values, at, (HALF, 128))], axis=1
        )

    upper = send(queries[HALF:], Y_LO)

    def q_piece(d):
        return lax.dynamic_slice(queries, (0, d * 256), (512, 256))

    got = [send(kv_piece(z ^ k), TO_HEAD[k]) for k in range(4)]
    *got, upper = lax.optimization_barrier(tuple(got) + (upper,))
    queries = jnp.concatenate([queries[:HALF], upper], axis=0)
    q_got = []
    got = jnp.stack(got)
    a0 = jnp.stack([pick(got, mine_d ^ plane) for plane in range(4)])

    b0 = send(a0, Y_LO)
    a1 = send(a0, X_DOWN)
    a3 = send(a0, X_UP)
    q_got = jnp.stack(q_got + [send(q_piece(z ^ k), TO_HEAD[k]) for k in range(0, 4)])
    q = jnp.stack(
        [jnp.stack([pick(q_got, mine_d ^ plane)[at : at + HALF] for plane in range(4)]) for at in (0, HALF)]
    )
    b0, a1, a3, q = lax.optimization_barrier((b0, a1, a3, q))
    near = jnp.stack([a0, a1, a3, b0])
    near_other = send(near, CORE)
    a2 = send(a1, X_DOWN)
    b3 = send(b0, X_UP)
    b1 = send(a1, Y_LO)
    b2 = send(b0, X_TWO)
    here, there = y_lo * 4, (1 - y_lo) * 4
    near_info = jnp.stack([here + x, here + (x + 1) % 4, here + (x + 3) % 4, there + x, j, core, 1 - y_hi]).astype(jnp.int32)
    far_info = jnp.stack(
        [there + (x + 1) % 4, there + (x + 3) % 4, here + (x + 2) % 4, there + (x + 2) % 4, j, core, 1 - y_hi]
    ).astype(jnp.int32)
    flag = jax.ShapeDtypeStruct((2,), jnp.int32)
    wide = jax.ShapeDtypeStruct((4, 512, 128), jnp.float32)
    narrow = jax.ShapeDtypeStruct((4, 256, 256), jnp.bfloat16)
    state = kernel_call(
        near_kernel, "attend_near", 1, HALF, (flag, wide, wide, wide, wide), (1, 0, 0, 0, 0),
        (near_info, ends, lo, hi, q, near, near_other), 4,
    )
    b1, b3, a2, b2, *state = lax.optimization_barrier((b1, b3, a2, b2) + tuple(state))
    flags, acc_ahead, acc_own, l_ahead, l_own = state
    far = jnp.stack([b1, b3, a2, b2])
    far_other = send(far, CORE)
    out_ahead, flags = kernel_call(
        functools.partial(far_kernel, True), "attend_ahead", 2, HALF, (narrow, flag), (0, 1),
        (far_info, ends, lo, hi, flags, q, far, far_other, acc_ahead, l_ahead), 5,
    )

    def send_home(out, pairs):
        return tuple(send(pick(out, mine_d ^ k), pairs[k]) for k in range(4))

    back_ahead = send_home(out_ahead, AHEAD_HOME)
    (out_own,) = kernel_call(
        functools.partial(far_kernel, False), "attend_own", 2, HALF, (narrow,), (0,),
        (far_info, ends, lo, hi, flags, q, far, far_other, acc_own, l_own), 5,
    )
    *back_ahead, out_own = lax.optimization_barrier(back_ahead + (out_own,))

    def project(back):
        back = jnp.stack(back)
        attended = jnp.concatenate([pick(back, z ^ d) for d in range(4)], axis=1)
        part = jnp.dot(attended, out_weight, preferred_element_type=jnp.float32).astype(jnp.bfloat16)
        part = part.reshape(2, 128, 4096)
        arrived = send(pick(part, 1 - core), CORE)
        return pick(part, core).astype(jnp.float32) + arrived.astype(jnp.float32)

    ahead, out_own = lax.optimization_barrier((project(back_ahead).astype(jnp.bfloat16), out_own))
    far_sum = send(ahead, Y_HI)
    back_own = send_home(out_own, OWN_HOME)
    return (project(back_own) + far_sum.astype(jnp.float32)).astype(jnp.bfloat16)


def solution(mesh):
    return jax.shard_map(
        on_device,
        mesh=mesh,
        in_specs=(P("ctx", "kv"), P("ctx", "kv"), P("ctx", "kv"), P(), P("kv", None)),
        out_specs=P(("ctx", "kv"), None),
        check_vma=False,
    )
```

```python
import functools
import math

import jax
import jax.numpy as jnp
from jax import lax
from jax.experimental import pallas as pl
from jax.experimental.pallas import tpu as pltpu
from jax.sharding import PartitionSpec as P

HEAD_WIDTH = 128
NEG = -1e30
AXES = ("ctx", "kv")
SCALE2 = HEAD_WIDTH ** -0.5 * math.log2(math.e)
HALF = 256
ROWS = 512
SAFE = 60.0 * math.log2(math.e)


def device_at(z, y_hi, y_lo, x, c):
    return ((z % 4) * 8 + y_lo * 4 + x % 4) * 4 + y_hi * 2 + c


def permutation(move):
    pairs = []
    for i in range(128):
        ctx, kv = divmod(i, 4)
        pairs.append((i, device_at(*move(ctx // 8, kv // 2, ctx // 4 % 2, ctx % 4, kv % 2))))
    return pairs


X_UP = permutation(lambda z, yh, yl, x, c: (z, yh, yl, x + 1, c))
X_TWO = permutation(lambda z, yh, yl, x, c: (z, yh, yl, x + 2, c))
X_DOWN = permutation(lambda z, yh, yl, x, c: (z, yh, yl, x + 3, c))
Y_LO = permutation(lambda z, yh, yl, x, c: (z, yh, 1 - yl, x, c))
Y_HI = permutation(lambda z, yh, yl, x, c: (z, 1 - yh, yl, x, c))
CORE = permutation(lambda z, yh, yl, x, c: (z, yh, yl, x, 1 - c))
TO_HEAD = [
    permutation(lambda z, yh, yl, x, c, k=k: (2 * c + (z ^ k) // 2, yh, yl, x, (z ^ k) % 2))
    for k in range(4)
]
TO_HOME = [[(b, a) for a, b in pairs] for pairs in TO_HEAD]


def send(x, pairs):
    return lax.ppermute(x, AXES, pairs)


def dot_nt(a, b):
    return lax.dot_general(a, b, (((1,), (1,)), ((), ())), preferred_element_type=jnp.float32)


def fold(p):
    total = p[:, :128]
    for at in range(128, p.shape[1], 128):
        total += p[:, at : at + 128]
    return total


def no_reference_needed(q_ref, mine_ref, other_ref):
    ones = jnp.ones((128, 128), jnp.bfloat16)

    def top_square(block):
        return jnp.max(jnp.dot(block * block, ones, preferred_element_type=jnp.float32), axis=0, keepdims=True)

    def k_top(i, top):
        a = top_square(mine_ref[i, :, :, :128].reshape(1024, 128))
        b = top_square(other_ref[i, :, :, :128].reshape(1024, 128))
        return jnp.maximum(top, jnp.maximum(a, b))

    def q_top(i, top):
        rows = pl.ds(pl.multiple_of(i * ROWS, ROWS), ROWS)
        return jnp.maximum(top, jnp.maximum(top_square(q_ref[rows, :128]), top_square(q_ref[rows, 128:])))

    zero = jnp.zeros((1, 128), jnp.float32)
    bound = lax.fori_loop(0, 4, k_top, zero) * lax.fori_loop(0, 4, q_top, zero)
    return jnp.max(bound) * 1.02 * SCALE2 * SCALE2 <= SAFE * SAFE


def attend_blocks(tile, first_pos, info_ref, ends_ref, lo, hi, safe, mine_ref, other_ref, q_s, acc, m_s, l_s, start_s, keep_s, undo):
    core = info_ref[5]

    @pl.when(lo == hi)
    def _():
        start_s[...] = jnp.full_like(start_s, lo)
        keep_s[...] = jnp.ones_like(keep_s)

    @pl.when(lo != hi)
    def _():
        q_pos = first_pos + lax.broadcasted_iota(jnp.int32, (tile, 128), 0)
        start = jnp.zeros((tile, 128), jnp.int32)
        for doc in range(16):
            end = ends_ref[doc]
            start = jnp.maximum(start, jnp.where(q_pos >= end, end, 0))
        start_s[...] = start
        keep = jnp.where(start <= lo, 1.0, 0.0)
        keep_s[...] = jnp.concatenate([keep, keep], axis=0)

    def keys_values(slot, zk):
        k_all = jnp.concatenate([mine_ref[slot, zk, :, :128], other_ref[slot, zk, :, :128]], axis=0)
        v_all = jnp.concatenate([mine_ref[slot, zk, :, 128:], other_ref[slot, zk, :, 128:]], axis=0)
        return k_all, v_all

    def mask_of(gk):
        column = lax.broadcasted_iota(jnp.int32, (tile, 512), 1)
        k_pos = gk * 512 + jnp.where(core == 0, column, column ^ 256)
        q_at = first_pos + lax.broadcasted_iota(jnp.int32, (tile, 512), 0)
        return (k_pos <= q_at) & (k_pos >= start_s[:, :1])

    parts = [slice(0, tile), slice(tile, 2 * tile)] if tile == ROWS else [slice(0, 2 * tile)]

    def quick(slot, zk, gk, masked):
        k_all, v_all = keys_values(slot, zk)
        if masked:
            allowed = mask_of(gk)
            if tile < ROWS:
                allowed = jnp.concatenate([allowed, allowed], axis=0)
        for part in parts:
            p = jnp.exp2(dot_nt(q_s[part, :], k_all) * SCALE2)
            if masked:
                p = jnp.where(allowed, p, 0.0)
            l_s[part, :] += fold(p)
            acc[part, :] += jnp.dot(p.astype(jnp.bfloat16), v_all, preferred_element_type=jnp.float32)

    def quick_two(slot_a, zk_a, slot_b, zk_b):
        k_a, v_a = keys_values(slot_a, zk_a)
        k_b, v_b = keys_values(slot_b, zk_b)
        scores = [(dot_nt(q_s[part, :], k_a), dot_nt(q_s[part, :], k_b)) for part in parts]
        for part, (s_a, s_b) in zip(parts, scores):
            p_a = jnp.exp2(s_a * SCALE2)
            p_b = jnp.exp2(s_b * SCALE2)
            l_s[part, :] += fold(p_a) + fold(p_b)
            acc[part, :] += jnp.dot(
                p_a.astype(jnp.bfloat16), v_a, preferred_element_type=jnp.float32
            ) + jnp.dot(p_b.astype(jnp.bfloat16), v_b, preferred_element_type=jnp.float32)

    def careful(slot, zk, gk):
        k_all, v_all = keys_values(slot, zk)
        allowed = mask_of(gk)
        for h in range(2):
            part = slice(h * tile, (h + 1) * tile)
            s = jnp.where(allowed, dot_nt(q_s[part, :], k_all), NEG)
            m_old = m_s[part, :]
            m_new = jnp.maximum(m_old, jnp.max(s, axis=1, keepdims=True))
            shrink = jnp.exp2((m_old - m_new) * SCALE2)
            p = jnp.where(allowed, jnp.exp2((s - m_new[:, :1]) * SCALE2), 0.0)
            m_s[part, :] = m_new
            l_s[part, :] = l_s[part, :] * shrink + fold(p)
            acc[part, :] = acc[part, :] * shrink + jnp.dot(
                p.astype(jnp.bfloat16), v_all, preferred_element_type=jnp.float32
            )

    def classify(kb):
        slot = kb // 4
        zk = kb % 4
        gk = zk * 8 + info_ref[slot]
        needed = (gk * 512 <= first_pos + tile - 1) & (gk * 512 + 511 >= lo)
        full = (gk * 512 + 511 < first_pos) & (gk * 512 >= lo)
        return slot, zk, gk, needed, full

    def whole_pair(i, carry):
        kb = i // 4 * 8 + i % 4
        a, b = classify(kb), classify(kb + 4)

        @pl.when(a[4] & b[4])
        def _():
            quick_two(a[0], a[1], b[0], b[1])

        @pl.when(a[4] & jnp.logical_not(b[4]))
        def _():
            quick(*a[:3], False)

        @pl.when(b[4] & jnp.logical_not(a[4]))
        def _():
            quick(*b[:3], False)

        return carry

    def edge(i, carry):
        diagonal, begin = first_pos // 512, lo // 512
        gk = jnp.where(i == 0, diagonal, begin)
        slot = jnp.int32(4)
        for at in range(4):
            slot = jnp.where(info_ref[at] == gk % 8, at, slot)
        due = (i == 0) | ((begin != diagonal) & (lo % 512 != 0))

        @pl.when(due & (slot < 4))
        def _():
            quick(slot, gk // 8, gk, True)

        return carry

    def any_block(kb, carry):
        slot, zk, gk, needed, _ = classify(kb)

        @pl.when(needed)
        def _():
            careful(slot, zk, gk)

        return carry

    @pl.when(safe)
    def _():
        lax.fori_loop(0, 8, whole_pair, 0)

        @pl.when(lo != hi)
        def _():
            undo(keep_s)

        lax.fori_loop(0, 2, edge, 0)

    @pl.when(jnp.logical_not(safe))
    def _():
        lax.fori_loop(0, 16, any_block, 0)


def near_kernel(info_ref, ends_ref, lo_ref, hi_ref, q_ref, mine_ref, other_ref, flag_ref, *refs):
    outs, (q_s, acc, m_s, l_s, start_s, keep_s) = refs[:4], refs[4:]
    safe = no_reference_needed(q_ref, mine_ref, other_ref)
    flag_ref[0] = jnp.where(safe, 1, 0)
    ahead = info_ref[6]

    def q_block(plane, carry):
        gq = (plane * 8 + info_ref[4]) * 2
        rows = pl.ds(pl.multiple_of(plane * ROWS, ROWS), ROWS)
        for h in range(2):
            q_s[h * ROWS : (h + 1) * ROWS, :] = q_ref[rows, h * 128 : (h + 1) * 128]
        acc[...] = jnp.zeros_like(acc)
        m_s[...] = jnp.full_like(m_s, NEG)
        l_s[...] = jnp.zeros_like(l_s)

        def undo(keep):
            acc[...] = acc[...] * keep[...]
            l_s[...] = l_s[...] * keep[...]

        attend_blocks(
            ROWS, gq * HALF, info_ref, ends_ref, lo_ref[gq], hi_ref[gq + 1], safe,
            mine_ref, other_ref, q_s, acc, m_s, l_s, start_s, keep_s, undo,
        )

        @pl.when(jnp.logical_not(safe))
        def _():
            lane = lax.broadcasted_iota(jnp.int32, l_s.shape, 1)
            l_s[...] = jnp.where(lane < 64, jnp.sum(l_s[...], axis=1, keepdims=True), m_s[...])

        at = pl.ds(pl.multiple_of(plane * HALF, HALF), HALF)
        for part, half in ((0, ahead), (1, 1 - ahead)):
            for h in range(2):
                rows_s = pl.ds(pl.multiple_of(h * ROWS + half * HALF, HALF), HALF)
                outs[part][at, h * 128 : (h + 1) * 128] = acc[rows_s, :]
                outs[2 + part][at, h * 128 : (h + 1) * 128] = l_s[rows_s, :]
        return carry

    lax.fori_loop(0, 4, q_block, 0)


def far_kernel(ahead, info_ref, ends_ref, lo_ref, hi_ref, flag_in, q_ref, mine_ref, other_ref, acc_in, l_in, *refs):
    near_safe = flag_in[0] == 1
    if ahead:
        out_ref, flag_ref, q_s, acc, m_s, l_s, start_s, keep_s = refs
        safe = near_safe & no_reference_needed(q_ref, mine_ref, other_ref)
        flag_ref[0] = jnp.where(near_safe, 1, 0)
        flag_ref[1] = jnp.where(safe, 1, 0)
        half = info_ref[6]
    else:
        out_ref, q_s, acc, m_s, l_s, start_s, keep_s = refs
        safe = flag_in[1] == 1
        half = 1 - info_ref[6]

    def q_block(plane, carry):
        gq = (plane * 8 + info_ref[4]) * 2 + half
        rows = pl.ds(pl.multiple_of(plane * ROWS + half * HALF, HALF), HALF)
        at = pl.ds(pl.multiple_of(plane * HALF, HALF), HALF)
        for h in range(2):
            part, cols = slice(h * HALF, (h + 1) * HALF), slice(h * 128, (h + 1) * 128)
            q_s[part, :] = q_ref[rows, cols]
            acc[part, :] = acc_in[at, cols]
            l_s[part, :] = l_in[at, cols]

        @pl.when(jnp.logical_not(safe))
        def _():
            lane = lax.broadcasted_iota(jnp.int32, l_s.shape, 1)
            old = l_s[...]
            total = jnp.sum(old, axis=1, keepdims=True)
            row_sum = jnp.where(near_safe, total, old[:, :1])
            reference = jnp.where(near_safe, jnp.where(total > 0.0, 0.0, NEG), old[:, 64:65])
            l_s[...] = jnp.where(lane == 0, row_sum, 0.0)
            m_s[...] = jnp.broadcast_to(reference, m_s.shape)

        def undo(keep):
            for h in range(2):
                part, cols = slice(h * HALF, (h + 1) * HALF), slice(h * 128, (h + 1) * 128)
                kept = keep[part, :] > 0.0
                acc[part, :] = jnp.where(kept, acc[part, :], acc_in[at, cols])
                l_s[part, :] = jnp.where(kept, l_s[part, :], l_in[at, cols])

        attend_blocks(
            HALF, gq * HALF, info_ref, ends_ref, lo_ref[gq], hi_ref[gq], safe,
            mine_ref, other_ref, q_s, acc, m_s, l_s, start_s, keep_s, undo,
        )
        for h in range(2):
            part, cols = slice(h * HALF, (h + 1) * HALF), slice(h * 128, (h + 1) * 128)
            total = jnp.sum(l_s[part, :], axis=1, keepdims=True)
            out_ref[at, cols] = (acc[part, :] / total).astype(jnp.bfloat16)
        return carry

    lax.fori_loop(0, 4, q_block, 0)


def kernel_call(kernel, name, share, tile, outs, out_flags, args, scalars):
    whole = pl.BlockSpec(memory_space=pltpu.VMEM)
    scalar = pl.BlockSpec(memory_space=pltpu.SMEM)
    return pl.pallas_call(
        kernel,
        out_shape=outs,
        in_specs=[scalar] * scalars + [whole] * (len(args) - scalars),
        out_specs=tuple(scalar if flag else whole for flag in out_flags),
        scratch_shapes=[pltpu.VMEM((2 * tile, 128), jnp.bfloat16)]
        + [pltpu.VMEM((2 * tile, 128), jnp.float32)] * 3
        + [pltpu.VMEM((tile, 128), jnp.int32), pltpu.VMEM((2 * tile, 128), jnp.float32)],
        compiler_params=pltpu.CompilerParams(vmem_limit_bytes=40 * 1024 * 1024),
        cost_estimate=pl.CostEstimate(
            flops=12_000_000_000 // share, bytes_accessed=8 * 1024 * 1024, transcendentals=12_000_000 // share
        ),
        name=name,
    )(*args)


def pick(stacked, index):
    return lax.dynamic_index_in_dim(stacked, index, 0, keepdims=False)


def on_device(queries, keys, values, doc_lengths, out_weight):
    ctx = lax.axis_index("ctx")
    kv = lax.axis_index("kv")
    z, y_lo, x = ctx // 8, ctx // 4 % 2, ctx % 4
    y_hi, core = kv // 2, kv % 2
    j = ctx % 8
    mine_d = 2 * (z % 2) + core
    ends = jnp.cumsum(doc_lengths).astype(jnp.int32)
    blocks = jnp.arange(64, dtype=jnp.int32) * HALF

    def start_of(position):
        return jnp.max(jnp.where(ends[None, :] <= position[:, None], ends[None, :], 0), axis=1)

    lo, hi = start_of(blocks), start_of(blocks + HALF - 1)

    def kv_piece(d):
        at = (d % 2 * HALF, d // 2 * 128)
        return jnp.concatenate(
            [lax.dynamic_slice(keys, at, (HALF, 128)), lax.dynamic_slice(values, at, (HALF, 128))], axis=1
        )

    def q_piece(d):
        return lax.dynamic_slice(queries, (0, d * 256), (512, 256))

    got = [send(kv_piece(z ^ k), TO_HEAD[k]) for k in range(4)]
    q_got = [send(q_piece(z ^ k), TO_HEAD[k]) for k in range(0)]
    *got, queries = lax.optimization_barrier(tuple(got) + tuple(q_got) + (queries,))
    got, q_got = got[:4], got[4:]
    got = jnp.stack(got)
    a0 = jnp.stack([pick(got, mine_d ^ plane) for plane in range(4)])

    b0 = send(a0, Y_LO)
    a1 = send(a0, X_DOWN)
    a3 = send(a0, X_UP)
    q_got = jnp.stack(q_got + [send(q_piece(z ^ k), TO_HEAD[k]) for k in range(0, 4)])
    q = jnp.concatenate([pick(q_got, mine_d ^ plane) for plane in range(4)], axis=0)
    b0, a1, a3, q = lax.optimization_barrier((b0, a1, a3, q))
    near = jnp.stack([a0, a1, a3, b0])
    near_other = send(near, CORE)
    a2 = send(a1, X_DOWN)
    b3 = send(b0, X_UP)
    b1 = send(a1, Y_LO)
    b2 = send(b0, X_TWO)
    here, there = y_lo * 4, (1 - y_lo) * 4
    near_info = jnp.stack([here + x, here + (x + 1) % 4, here + (x + 3) % 4, there + x, j, core, 1 - y_hi]).astype(jnp.int32)
    far_info = jnp.stack(
        [there + (x + 1) % 4, there + (x + 3) % 4, here + (x + 2) % 4, there + (x + 2) % 4, j, core, 1 - y_hi]
    ).astype(jnp.int32)
    flag = jax.ShapeDtypeStruct((2,), jnp.int32)
    wide = jax.ShapeDtypeStruct((1024, 256), jnp.float32)
    narrow = jax.ShapeDtypeStruct((1024, 256), jnp.bfloat16)
    state = kernel_call(
        near_kernel, "attend_near", 1, ROWS, (flag, wide, wide, wide, wide), (1, 0, 0, 0, 0),
        (near_info, ends, lo, hi, q, near, near_other), 4,
    )
    b1, b3, a2, b2, *state = lax.optimization_barrier((b1, b3, a2, b2) + tuple(state))
    flags, acc_ahead, acc_own, l_ahead, l_own = state
    far = jnp.stack([b1, b3, a2, b2])
    far_other = send(far, CORE)
    out_ahead, flags = kernel_call(
        functools.partial(far_kernel, True), "attend_ahead", 2, HALF, (narrow, flag), (0, 1),
        (far_info, ends, lo, hi, flags, q, far, far_other, acc_ahead, l_ahead), 5,
    )

    def send_home(out):
        planes = out.reshape(4, 256, 256)
        return tuple(send(pick(planes, mine_d ^ k), TO_HOME[k]) for k in range(4))

    back_ahead = send_home(out_ahead)
    (out_own,) = kernel_call(
        functools.partial(far_kernel, False), "attend_own", 2, HALF, (narrow,), (0,),
        (far_info, ends, lo, hi, flags, q, far, far_other, acc_own, l_own), 5,
    )
    *back_ahead, out_own = lax.optimization_barrier(back_ahead + (out_own,))

    def partial(back):
        back = jnp.stack(back)
        attended = jnp.concatenate([pick(back, z ^ d) for d in range(4)], axis=1)
        part = jnp.dot(attended, out_weight, preferred_element_type=jnp.float32).astype(jnp.bfloat16)
        part = part.reshape(2, 128, 4096)
        return pick(part, core), send(pick(part, 1 - core), CORE)

    kept, arrived = partial(back_ahead)
    ahead = (kept.astype(jnp.float32) + arrived.astype(jnp.float32)).astype(jnp.bfloat16)
    ahead, out_own = lax.optimization_barrier((ahead, out_own))
    far_sum = send(ahead, Y_HI)

    def own_rows(out):
        return partial(send_home(out))

    def no_rows(out):
        return jnp.zeros((128, 4096), jnp.bfloat16), jnp.zeros((128, 4096), jnp.bfloat16)

    kept, arrived = lax.cond(doc_lengths[0] > 0, own_rows, no_rows, out_own)
    total = kept.astype(jnp.float32) + arrived.astype(jnp.float32) + far_sum.astype(jnp.float32)
    return total.astype(jnp.bfloat16)


def solution(mesh):
    return jax.shard_map(
        on_device,
        mesh=mesh,
        in_specs=(P("ctx", "kv"), P("ctx", "kv"), P("ctx", "kv"), P(), P("kv", None)),
        out_specs=P(("ctx", "kv"), None),
        check_vma=False,
    )
```

```python
import functools
import math

import jax
import jax.numpy as jnp
from jax import lax
from jax.experimental import pallas as pl
from jax.experimental.pallas import tpu as pltpu
from jax.sharding import PartitionSpec as P

HEAD_WIDTH = 128
NEG = -1e30
AXES = ("ctx", "kv")
SCALE2 = HEAD_WIDTH ** -0.5 * math.log2(math.e)
HALF = 256
ROWS = 512
SAFE = 60.0 * math.log2(math.e)


def device_at(z, y_hi, y_lo, x, c):
    return ((z % 4) * 8 + y_lo * 4 + x % 4) * 4 + y_hi * 2 + c


def permutation(move):
    pairs = []
    for i in range(128):
        ctx, kv = divmod(i, 4)
        pairs.append((i, device_at(*move(ctx // 8, kv // 2, ctx // 4 % 2, ctx % 4, kv % 2))))
    return pairs


X_UP = permutation(lambda z, yh, yl, x, c: (z, yh, yl, x + 1, c))
X_TWO = permutation(lambda z, yh, yl, x, c: (z, yh, yl, x + 2, c))
X_DOWN = permutation(lambda z, yh, yl, x, c: (z, yh, yl, x + 3, c))
Y_LO = permutation(lambda z, yh, yl, x, c: (z, yh, 1 - yl, x, c))
Y_HI = permutation(lambda z, yh, yl, x, c: (z, 1 - yh, yl, x, c))
CORE = permutation(lambda z, yh, yl, x, c: (z, yh, yl, x, 1 - c))
TO_HEAD = [
    permutation(lambda z, yh, yl, x, c, k=k: (2 * c + (z ^ k) // 2, yh, yl, x, (z ^ k) % 2))
    for k in range(4)
]
TO_HOME = [[(b, a) for a, b in pairs] for pairs in TO_HEAD]


def send(x, pairs):
    return lax.ppermute(x, AXES, pairs)


def dot_nt(a, b):
    return lax.dot_general(a, b, (((1,), (1,)), ((), ())), preferred_element_type=jnp.float32)


def fold(p):
    total = p[:, :128]
    for at in range(128, p.shape[1], 128):
        total += p[:, at : at + 128]
    return total


def no_reference_needed(q_ref, mine_ref, other_ref):
    ones = jnp.ones((128, 128), jnp.bfloat16)

    def top_square(block):
        return jnp.max(jnp.dot(block * block, ones, preferred_element_type=jnp.float32), axis=0, keepdims=True)

    def k_top(i, top):
        a = top_square(mine_ref[i, :, :, :128].reshape(1024, 128))
        b = top_square(other_ref[i, :, :, :128].reshape(1024, 128))
        return jnp.maximum(top, jnp.maximum(a, b))

    def q_top(i, top):
        rows = pl.ds(pl.multiple_of(i * ROWS, ROWS), ROWS)
        return jnp.maximum(top, jnp.maximum(top_square(q_ref[rows, :128]), top_square(q_ref[rows, 128:])))

    zero = jnp.zeros((1, 128), jnp.float32)
    bound = lax.fori_loop(0, 4, k_top, zero) * lax.fori_loop(0, 4, q_top, zero)
    return jnp.max(bound) * 1.02 * SCALE2 * SCALE2 <= SAFE * SAFE


def attend_blocks(tile, first_pos, info_ref, ends_ref, lo, hi, safe, mine_ref, other_ref, q_s, acc, m_s, l_s, start_s, keep_s, undo):
    core = info_ref[5]

    @pl.when(lo == hi)
    def _():
        start_s[...] = jnp.full_like(start_s, lo)
        keep_s[...] = jnp.ones_like(keep_s)

    @pl.when(lo != hi)
    def _():
        q_pos = first_pos + lax.broadcasted_iota(jnp.int32, (tile, 128), 0)
        start = jnp.zeros((tile, 128), jnp.int32)
        for doc in range(16):
            end = ends_ref[doc]
            start = jnp.maximum(start, jnp.where(q_pos >= end, end, 0))
        start_s[...] = start
        keep = jnp.where(start <= lo, 1.0, 0.0)
        keep_s[...] = jnp.concatenate([keep, keep], axis=0)

    def keys_values(slot, zk):
        k_all = jnp.concatenate([mine_ref[slot, zk, :, :128], other_ref[slot, zk, :, :128]], axis=0)
        v_all = jnp.concatenate([mine_ref[slot, zk, :, 128:], other_ref[slot, zk, :, 128:]], axis=0)
        return k_all, v_all

    def mask_of(gk):
        column = lax.broadcasted_iota(jnp.int32, (tile, 512), 1)
        k_pos = gk * 512 + jnp.where(core == 0, column, column ^ 256)
        q_at = first_pos + lax.broadcasted_iota(jnp.int32, (tile, 512), 0)
        return (k_pos <= q_at) & (k_pos >= start_s[:, :1])

    parts = [slice(0, tile), slice(tile, 2 * tile)] if tile == ROWS else [slice(0, 2 * tile)]

    def quick(slot, zk, gk, masked):
        k_all, v_all = keys_values(slot, zk)
        if masked:
            allowed = mask_of(gk)
            if tile < ROWS:
                allowed = jnp.concatenate([allowed, allowed], axis=0)
        for part in parts:
            p = jnp.exp2(dot_nt(q_s[part, :], k_all) * SCALE2)
            if masked:
                p = jnp.where(allowed, p, 0.0)
            l_s[part, :] += fold(p)
            acc[part, :] += jnp.dot(p.astype(jnp.bfloat16), v_all, preferred_element_type=jnp.float32)

    def quick_two(slot_a, zk_a, slot_b, zk_b):
        k_a, v_a = keys_values(slot_a, zk_a)
        k_b, v_b = keys_values(slot_b, zk_b)
        scores = [(dot_nt(q_s[part, :], k_a), dot_nt(q_s[part, :], k_b)) for part in parts]
        for part, (s_a, s_b) in zip(parts, scores):
            p_a = jnp.exp2(s_a * SCALE2)
            p_b = jnp.exp2(s_b * SCALE2)
            l_s[part, :] += fold(p_a) + fold(p_b)
            acc[part, :] += jnp.dot(
                p_a.astype(jnp.bfloat16), v_a, preferred_element_type=jnp.float32
            ) + jnp.dot(p_b.astype(jnp.bfloat16), v_b, preferred_element_type=jnp.float32)

    def careful(slot, zk, gk):
        k_all, v_all = keys_values(slot, zk)
        allowed = mask_of(gk)
        for h in range(2):
            part = slice(h * tile, (h + 1) * tile)
            s = jnp.where(allowed, dot_nt(q_s[part, :], k_all), NEG)
            m_old = m_s[part, :]
            m_new = jnp.maximum(m_old, jnp.max(s, axis=1, keepdims=True))
            shrink = jnp.exp2((m_old - m_new) * SCALE2)
            p = jnp.where(allowed, jnp.exp2((s - m_new[:, :1]) * SCALE2), 0.0)
            m_s[part, :] = m_new
            l_s[part, :] = l_s[part, :] * shrink + fold(p)
            acc[part, :] = acc[part, :] * shrink + jnp.dot(
                p.astype(jnp.bfloat16), v_all, preferred_element_type=jnp.float32
            )

    def classify(kb):
        slot = kb // 4
        zk = kb % 4
        gk = zk * 8 + info_ref[slot]
        needed = (gk * 512 <= first_pos + tile - 1) & (gk * 512 + 511 >= lo)
        full = (gk * 512 + 511 < first_pos) & (gk * 512 >= lo)
        return slot, zk, gk, needed, full

    def whole_pair(i, carry):
        kb = i // 4 * 8 + i % 4
        a, b = classify(kb), classify(kb + 4)

        @pl.when(a[4] & b[4])
        def _():
            quick_two(a[0], a[1], b[0], b[1])

        @pl.when(a[4] & jnp.logical_not(b[4]))
        def _():
            quick(*a[:3], False)

        @pl.when(b[4] & jnp.logical_not(a[4]))
        def _():
            quick(*b[:3], False)

        return carry

    def edge(i, carry):
        diagonal, begin = first_pos // 512, lo // 512
        gk = jnp.where(i == 0, diagonal, begin)
        slot = jnp.int32(4)
        for at in range(4):
            slot = jnp.where(info_ref[at] == gk % 8, at, slot)
        due = (i == 0) | ((begin != diagonal) & (lo % 512 != 0))

        @pl.when(due & (slot < 4))
        def _():
            quick(slot, gk // 8, gk, True)

        return carry

    def any_block(kb, carry):
        slot, zk, gk, needed, _ = classify(kb)

        @pl.when(needed)
        def _():
            careful(slot, zk, gk)

        return carry

    @pl.when(safe)
    def _():
        lax.fori_loop(0, 8, whole_pair, 0)

        @pl.when(lo != hi)
        def _():
            undo(keep_s)

        lax.fori_loop(0, 2, edge, 0)

    @pl.when(jnp.logical_not(safe))
    def _():
        lax.fori_loop(0, 16, any_block, 0)


def near_kernel(info_ref, ends_ref, lo_ref, hi_ref, q_ref, mine_ref, other_ref, flag_ref, *refs):
    outs, (q_s, acc, m_s, l_s, start_s, keep_s) = refs[:4], refs[4:]
    safe = no_reference_needed(q_ref, mine_ref, other_ref)
    flag_ref[0] = jnp.where(safe, 1, 0)
    ahead = info_ref[6]

    def q_block(plane, carry):
        gq = (plane * 8 + info_ref[4]) * 2
        rows = pl.ds(pl.multiple_of(plane * ROWS, ROWS), ROWS)
        for h in range(2):
            q_s[h * ROWS : (h + 1) * ROWS, :] = q_ref[rows, h * 128 : (h + 1) * 128]
        acc[...] = jnp.zeros_like(acc)
        m_s[...] = jnp.full_like(m_s, NEG)
        l_s[...] = jnp.zeros_like(l_s)

        def undo(keep):
            acc[...] = acc[...] * keep[...]
            l_s[...] = l_s[...] * keep[...]

        attend_blocks(
            ROWS, gq * HALF, info_ref, ends_ref, lo_ref[gq], hi_ref[gq + 1], safe,
            mine_ref, other_ref, q_s, acc, m_s, l_s, start_s, keep_s, undo,
        )

        @pl.when(jnp.logical_not(safe))
        def _():
            lane = lax.broadcasted_iota(jnp.int32, l_s.shape, 1)
            l_s[...] = jnp.where(lane < 64, jnp.sum(l_s[...], axis=1, keepdims=True), m_s[...])

        at = pl.ds(pl.multiple_of(plane * HALF, HALF), HALF)
        for part, half in ((0, ahead), (1, 1 - ahead)):
            for h in range(2):
                rows_s = pl.ds(pl.multiple_of(h * ROWS + half * HALF, HALF), HALF)
                outs[part][at, h * 128 : (h + 1) * 128] = acc[rows_s, :]
                outs[2 + part][at, h * 128 : (h + 1) * 128] = l_s[rows_s, :]
        return carry

    lax.fori_loop(0, 4, q_block, 0)


def far_kernel(ahead, info_ref, ends_ref, lo_ref, hi_ref, flag_in, q_ref, mine_ref, other_ref, acc_in, l_in, *refs):
    near_safe = flag_in[0] == 1
    if ahead:
        out_ref, flag_ref, q_s, acc, m_s, l_s, start_s, keep_s = refs
        safe = near_safe & no_reference_needed(q_ref, mine_ref, other_ref)
        flag_ref[0] = jnp.where(near_safe, 1, 0)
        flag_ref[1] = jnp.where(safe, 1, 0)
        half = info_ref[6]
    else:
        out_ref, q_s, acc, m_s, l_s, start_s, keep_s = refs
        safe = flag_in[1] == 1
        half = 1 - info_ref[6]

    def q_block(plane, carry):
        gq = (plane * 8 + info_ref[4]) * 2 + half
        rows = pl.ds(pl.multiple_of(plane * ROWS + half * HALF, HALF), HALF)
        at = pl.ds(pl.multiple_of(plane * HALF, HALF), HALF)
        for h in range(2):
            part, cols = slice(h * HALF, (h + 1) * HALF), slice(h * 128, (h + 1) * 128)
            q_s[part, :] = q_ref[rows, cols]
            acc[part, :] = acc_in[at, cols]
            l_s[part, :] = l_in[at, cols]

        @pl.when(jnp.logical_not(safe))
        def _():
            lane = lax.broadcasted_iota(jnp.int32, l_s.shape, 1)
            old = l_s[...]
            total = jnp.sum(old, axis=1, keepdims=True)
            row_sum = jnp.where(near_safe, total, old[:, :1])
            reference = jnp.where(near_safe, jnp.where(total > 0.0, 0.0, NEG), old[:, 64:65])
            l_s[...] = jnp.where(lane == 0, row_sum, 0.0)
            m_s[...] = jnp.broadcast_to(reference, m_s.shape)

        def undo(keep):
            for h in range(2):
                part, cols = slice(h * HALF, (h + 1) * HALF), slice(h * 128, (h + 1) * 128)
                kept = keep[part, :] > 0.0
                acc[part, :] = jnp.where(kept, acc[part, :], acc_in[at, cols])
                l_s[part, :] = jnp.where(kept, l_s[part, :], l_in[at, cols])

        attend_blocks(
            HALF, gq * HALF, info_ref, ends_ref, lo_ref[gq], hi_ref[gq], safe,
            mine_ref, other_ref, q_s, acc, m_s, l_s, start_s, keep_s, undo,
        )
        for h in range(2):
            part, cols = slice(h * HALF, (h + 1) * HALF), slice(h * 128, (h + 1) * 128)
            total = jnp.sum(l_s[part, :], axis=1, keepdims=True)
            out_ref[at, cols] = (acc[part, :] / total).astype(jnp.bfloat16)
        return carry

    lax.fori_loop(0, 4, q_block, 0)


def kernel_call(kernel, name, share, tile, outs, out_flags, args, scalars):
    whole = pl.BlockSpec(memory_space=pltpu.VMEM)
    scalar = pl.BlockSpec(memory_space=pltpu.SMEM)
    return pl.pallas_call(
        kernel,
        out_shape=outs,
        in_specs=[scalar] * scalars + [whole] * (len(args) - scalars),
        out_specs=tuple(scalar if flag else whole for flag in out_flags),
        scratch_shapes=[pltpu.VMEM((2 * tile, 128), jnp.bfloat16)]
        + [pltpu.VMEM((2 * tile, 128), jnp.float32)] * 3
        + [pltpu.VMEM((tile, 128), jnp.int32), pltpu.VMEM((2 * tile, 128), jnp.float32)],
        compiler_params=pltpu.CompilerParams(vmem_limit_bytes=40 * 1024 * 1024),
        cost_estimate=pl.CostEstimate(
            flops=12_000_000_000 // share, bytes_accessed=8 * 1024 * 1024, transcendentals=12_000_000 // share
        ),
        name=name,
    )(*args)


def pick(stacked, index):
    return lax.dynamic_index_in_dim(stacked, index, 0, keepdims=False)


def on_device(queries, keys, values, doc_lengths, out_weight):
    ctx = lax.axis_index("ctx")
    kv = lax.axis_index("kv")
    z, y_lo, x = ctx // 8, ctx // 4 % 2, ctx % 4
    y_hi, core = kv // 2, kv % 2
    j = ctx % 8
    mine_d = 2 * (z % 2) + core
    ends = jnp.cumsum(doc_lengths).astype(jnp.int32)
    blocks = jnp.arange(64, dtype=jnp.int32) * HALF

    def start_of(position):
        return jnp.max(jnp.where(ends[None, :] <= position[:, None], ends[None, :], 0), axis=1)

    lo, hi = start_of(blocks), start_of(blocks + HALF - 1)

    def kv_piece(d):
        at = (d % 2 * HALF, d // 2 * 128)
        return jnp.concatenate(
            [lax.dynamic_slice(keys, at, (HALF, 128)), lax.dynamic_slice(values, at, (HALF, 128))], axis=1
        )

    def q_piece(d):
        return lax.dynamic_slice(queries, (0, d * 256), (512, 256))

    got = [send(kv_piece(z ^ k), TO_HEAD[k]) for k in range(4)]
    got = jnp.stack(got)
    a0 = jnp.stack([pick(got, mine_d ^ plane) for plane in range(4)])

    b0 = send(a0, Y_LO)
    a1 = send(a0, X_DOWN)
    a3 = send(a0, X_UP)
    q_got = jnp.stack([send(q_piece(z ^ k), TO_HEAD[k]) for k in range(4)])
    q = jnp.concatenate([pick(q_got, mine_d ^ plane) for plane in range(4)], axis=0)
    b0, a1, a3, q = lax.optimization_barrier((b0, a1, a3, q))
    near = jnp.stack([a0, a1, a3, b0])
    near_other = send(near, CORE)
    a2 = send(a1, X_DOWN)
    b3 = send(b0, X_UP)
    b1 = send(a1, Y_LO)
    b2 = send(b0, X_TWO)
    here, there = y_lo * 4, (1 - y_lo) * 4
    near_info = jnp.stack([here + x, here + (x + 1) % 4, here + (x + 3) % 4, there + x, j, core, 1 - y_hi]).astype(jnp.int32)
    far_info = jnp.stack(
        [there + (x + 1) % 4, there + (x + 3) % 4, here + (x + 2) % 4, there + (x + 2) % 4, j, core, 1 - y_hi]
    ).astype(jnp.int32)
    flag = jax.ShapeDtypeStruct((2,), jnp.int32)
    wide = jax.ShapeDtypeStruct((1024, 256), jnp.float32)
    narrow = jax.ShapeDtypeStruct((1024, 256), jnp.bfloat16)
    state = kernel_call(
        near_kernel, "attend_near", 1, ROWS, (flag, wide, wide, wide, wide), (1, 0, 0, 0, 0),
        (near_info, ends, lo, hi, q, near, near_other), 4,
    )
    flags, acc_ahead, acc_own, l_ahead, l_own = state
    b1, b3, a2, b2, flags = lax.optimization_barrier((b1, b3, a2, b2, flags))
    far = jnp.stack([b1, b3, a2, b2])
    far_other = send(far, CORE)
    out_ahead, flags = kernel_call(
        functools.partial(far_kernel, True), "attend_ahead", 2, HALF, (narrow, flag), (0, 1),
        (far_info, ends, lo, hi, flags, q, far, far_other, acc_ahead, l_ahead), 5,
    )

    def send_home(out):
        planes = out.reshape(4, 256, 256)
        return tuple(send(pick(planes, mine_d ^ k), TO_HOME[k]) for k in range(4))

    back_ahead = send_home(out_ahead)
    (out_own,) = kernel_call(
        functools.partial(far_kernel, False), "attend_own", 2, HALF, (narrow,), (0,),
        (far_info, ends, lo, hi, flags, q, far, far_other, acc_own, l_own), 5,
    )
    *back_ahead, out_own = lax.optimization_barrier(back_ahead + (out_own,))

    def partial(back):
        back = jnp.stack(back)
        attended = jnp.concatenate([pick(back, z ^ d) for d in range(4)], axis=1)
        part = jnp.dot(attended, out_weight, preferred_element_type=jnp.float32).astype(jnp.bfloat16)
        part = part.reshape(2, 128, 4096)
        return pick(part, core), send(pick(part, 1 - core), CORE)

    kept, arrived = partial(back_ahead)
    ahead = (kept.astype(jnp.float32) + arrived.astype(jnp.float32)).astype(jnp.bfloat16)
    ahead, out_own = lax.optimization_barrier((ahead, out_own))
    far_sum = send(ahead, Y_HI)

    def own_rows(out):
        return partial(send_home(out))

    def no_rows(out):
        return jnp.zeros((128, 4096), jnp.bfloat16), jnp.zeros((128, 4096), jnp.bfloat16)

    kept, arrived = lax.cond(doc_lengths[0] > 0, own_rows, no_rows, out_own)
    total = kept.astype(jnp.float32) + arrived.astype(jnp.float32) + far_sum.astype(jnp.float32)
    return total.astype(jnp.bfloat16)


def solution(mesh):
    return jax.shard_map(
        on_device,
        mesh=mesh,
        in_specs=(P("ctx", "kv"), P("ctx", "kv"), P("ctx", "kv"), P(), P("kv", None)),
        out_specs=P(("ctx", "kv"), None),
        check_vma=False,
    )
```

```python
import functools
import math

import jax
import jax.numpy as jnp
from jax import lax
from jax.experimental import pallas as pl
from jax.experimental.pallas import tpu as pltpu
from jax.sharding import PartitionSpec as P

HEAD_WIDTH = 128
NEG = -1e30
AXES = ("ctx", "kv")
SCALE2 = HEAD_WIDTH ** -0.5 * math.log2(math.e)
HALF = 256
ROWS = 512
SAFE = 60.0 * math.log2(math.e)


def device_at(z, y_hi, y_lo, x, c):
    return ((z % 4) * 8 + y_lo * 4 + x % 4) * 4 + y_hi * 2 + c


def permutation(move):
    pairs = []
    for i in range(128):
        ctx, kv = divmod(i, 4)
        pairs.append((i, device_at(*move(ctx // 8, kv // 2, ctx // 4 % 2, ctx % 4, kv % 2))))
    return pairs


X_UP = permutation(lambda z, yh, yl, x, c: (z, yh, yl, x + 1, c))
X_TWO = permutation(lambda z, yh, yl, x, c: (z, yh, yl, x + 2, c))
X_DOWN = permutation(lambda z, yh, yl, x, c: (z, yh, yl, x + 3, c))
Y_LO = permutation(lambda z, yh, yl, x, c: (z, yh, 1 - yl, x, c))
Y_HI = permutation(lambda z, yh, yl, x, c: (z, 1 - yh, yl, x, c))
CORE = permutation(lambda z, yh, yl, x, c: (z, yh, yl, x, 1 - c))
TO_HEAD = [
    permutation(lambda z, yh, yl, x, c, k=k: (2 * c + (z ^ k) // 2, yh, yl, x, (z ^ k) % 2))
    for k in range(4)
]
TO_HOME = [[(b, a) for a, b in pairs] for pairs in TO_HEAD]


def send(x, pairs):
    return lax.ppermute(x, AXES, pairs)


def dot_nt(a, b):
    return lax.dot_general(a, b, (((1,), (1,)), ((), ())), preferred_element_type=jnp.float32)


def fold(p):
    total = p[:, :128]
    for at in range(128, p.shape[1], 128):
        total += p[:, at : at + 128]
    return total


def no_reference_needed(q_ref, mine_ref, other_ref):
    ones = jnp.ones((128, 128), jnp.bfloat16)

    def top_square(block):
        return jnp.max(jnp.dot(block * block, ones, preferred_element_type=jnp.float32), axis=0, keepdims=True)

    def k_top(i, top):
        a = top_square(mine_ref[i, :, :, :128].reshape(1024, 128))
        b = top_square(other_ref[i, :, :, :128].reshape(1024, 128))
        return jnp.maximum(top, jnp.maximum(a, b))

    def q_top(i, top):
        rows = pl.ds(pl.multiple_of(i * ROWS, ROWS), ROWS)
        return jnp.maximum(top, jnp.maximum(top_square(q_ref[rows, :128]), top_square(q_ref[rows, 128:])))

    zero = jnp.zeros((1, 128), jnp.float32)
    bound = lax.fori_loop(0, 4, k_top, zero) * lax.fori_loop(0, 4, q_top, zero)
    return jnp.max(bound) * 1.02 * SCALE2 * SCALE2 <= SAFE * SAFE


def attend_blocks(tile, first_pos, info_ref, ends_ref, lo, hi, safe, mine_ref, other_ref, q_s, acc, m_s, l_s, start_s, keep_s, undo):
    core = info_ref[5]

    @pl.when(lo == hi)
    def _():
        start_s[...] = jnp.full_like(start_s, lo)
        keep_s[...] = jnp.ones_like(keep_s)

    @pl.when(lo != hi)
    def _():
        q_pos = first_pos + lax.broadcasted_iota(jnp.int32, (tile, 128), 0)
        start = jnp.zeros((tile, 128), jnp.int32)
        for doc in range(16):
            end = ends_ref[doc]
            start = jnp.maximum(start, jnp.where(q_pos >= end, end, 0))
        start_s[...] = start
        keep = jnp.where(start <= lo, 1.0, 0.0)
        keep_s[...] = jnp.concatenate([keep, keep], axis=0)

    def keys_values(slot, zk):
        k_all = jnp.concatenate([mine_ref[slot, zk, :, :128], other_ref[slot, zk, :, :128]], axis=0)
        v_all = jnp.concatenate([mine_ref[slot, zk, :, 128:], other_ref[slot, zk, :, 128:]], axis=0)
        return k_all, v_all

    def mask_of(gk):
        column = lax.broadcasted_iota(jnp.int32, (tile, 512), 1)
        k_pos = gk * 512 + jnp.where(core == 0, column, column ^ 256)
        q_at = first_pos + lax.broadcasted_iota(jnp.int32, (tile, 512), 0)
        return (k_pos <= q_at) & (k_pos >= start_s[:, :1])

    parts = [slice(0, tile), slice(tile, 2 * tile)] if tile == ROWS else [slice(0, 2 * tile)]

    def quick(slot, zk, gk, masked):
        k_all, v_all = keys_values(slot, zk)
        if masked:
            allowed = mask_of(gk)
            if tile < ROWS:
                allowed = jnp.concatenate([allowed, allowed], axis=0)
        for part in parts:
            p = jnp.exp2(dot_nt(q_s[part, :], k_all) * SCALE2)
            if masked:
                p = jnp.where(allowed, p, 0.0)
            l_s[part, :] += fold(p)
            acc[part, :] += jnp.dot(p.astype(jnp.bfloat16), v_all, preferred_element_type=jnp.float32)

    def quick_two(slot_a, zk_a, slot_b, zk_b):
        k_a, v_a = keys_values(slot_a, zk_a)
        k_b, v_b = keys_values(slot_b, zk_b)
        scores = [(dot_nt(q_s[part, :], k_a), dot_nt(q_s[part, :], k_b)) for part in parts]
        for part, (s_a, s_b) in zip(parts, scores):
            p_a = jnp.exp2(s_a * SCALE2)
            p_b = jnp.exp2(s_b * SCALE2)
            l_s[part, :] += fold(p_a) + fold(p_b)
            acc[part, :] += jnp.dot(
                p_a.astype(jnp.bfloat16), v_a, preferred_element_type=jnp.float32
            ) + jnp.dot(p_b.astype(jnp.bfloat16), v_b, preferred_element_type=jnp.float32)

    def careful(slot, zk, gk):
        k_all, v_all = keys_values(slot, zk)
        allowed = mask_of(gk)
        for h in range(2):
            part = slice(h * tile, (h + 1) * tile)
            s = jnp.where(allowed, dot_nt(q_s[part, :], k_all), NEG)
            m_old = m_s[part, :]
            m_new = jnp.maximum(m_old, jnp.max(s, axis=1, keepdims=True))
            shrink = jnp.exp2((m_old - m_new) * SCALE2)
            p = jnp.where(allowed, jnp.exp2((s - m_new[:, :1]) * SCALE2), 0.0)
            m_s[part, :] = m_new
            l_s[part, :] = l_s[part, :] * shrink + fold(p)
            acc[part, :] = acc[part, :] * shrink + jnp.dot(
                p.astype(jnp.bfloat16), v_all, preferred_element_type=jnp.float32
            )

    def classify(kb):
        slot = kb // 4
        zk = kb % 4
        gk = zk * 8 + info_ref[slot]
        needed = (gk * 512 <= first_pos + tile - 1) & (gk * 512 + 511 >= lo)
        full = (gk * 512 + 511 < first_pos) & (gk * 512 >= lo)
        return slot, zk, gk, needed, full

    def whole_pair(i, carry):
        kb = i // 4 * 8 + i % 4
        a, b = classify(kb), classify(kb + 4)

        @pl.when(a[4] & b[4])
        def _():
            quick_two(a[0], a[1], b[0], b[1])

        @pl.when(a[4] & jnp.logical_not(b[4]))
        def _():
            quick(*a[:3], False)

        @pl.when(b[4] & jnp.logical_not(a[4]))
        def _():
            quick(*b[:3], False)

        return carry

    def edge(i, carry):
        diagonal, begin = first_pos // 512, lo // 512
        gk = jnp.where(i == 0, diagonal, begin)
        slot = jnp.int32(4)
        for at in range(4):
            slot = jnp.where(info_ref[at] == gk % 8, at, slot)
        due = (i == 0) | ((begin != diagonal) & (lo % 512 != 0))

        @pl.when(due & (slot < 4))
        def _():
            quick(slot, gk // 8, gk, True)

        return carry

    def any_block(kb, carry):
        slot, zk, gk, needed, _ = classify(kb)

        @pl.when(needed)
        def _():
            careful(slot, zk, gk)

        return carry

    @pl.when(safe)
    def _():
        lax.fori_loop(0, 8, whole_pair, 0)

        @pl.when(lo != hi)
        def _():
            undo(keep_s)

        lax.fori_loop(0, 2, edge, 0)

    @pl.when(jnp.logical_not(safe))
    def _():
        lax.fori_loop(0, 16, any_block, 0)


def near_kernel(alone, info_ref, ends_ref, lo_ref, hi_ref, *refs):
    if alone:
        flag_in, q_ref, mine_ref, other_ref, *refs = refs
        safe = flag_in[0] == 1
    else:
        q_ref, mine_ref, other_ref, flag_ref, *refs = refs
        safe = no_reference_needed(q_ref, mine_ref, other_ref)
        flag_ref[0] = jnp.where(safe, 1, 0)
    refs = tuple(refs)
    outs, (q_s, acc, m_s, l_s, start_s, keep_s) = refs[:4], refs[4:]
    ahead = info_ref[6]

    def q_block(i, carry):
        plane = 1 if alone else i + jnp.minimum(i, 1)
        gq = (plane * 8 + info_ref[4]) * 2
        rows = pl.ds(pl.multiple_of(plane * ROWS, ROWS), ROWS)
        for h in range(2):
            q_s[h * ROWS : (h + 1) * ROWS, :] = q_ref[rows, h * 128 : (h + 1) * 128]
        acc[...] = jnp.zeros_like(acc)
        m_s[...] = jnp.full_like(m_s, NEG)
        l_s[...] = jnp.zeros_like(l_s)

        def undo(keep):
            acc[...] = acc[...] * keep[...]
            l_s[...] = l_s[...] * keep[...]

        attend_blocks(
            ROWS, gq * HALF, info_ref, ends_ref, lo_ref[gq], hi_ref[gq + 1], safe,
            mine_ref, other_ref, q_s, acc, m_s, l_s, start_s, keep_s, undo,
        )

        @pl.when(jnp.logical_not(safe))
        def _():
            lane = lax.broadcasted_iota(jnp.int32, l_s.shape, 1)
            l_s[...] = jnp.where(lane < 64, jnp.sum(l_s[...], axis=1, keepdims=True), m_s[...])

        at = pl.ds(pl.multiple_of(i * HALF, HALF), HALF)
        for part, half in ((0, ahead), (1, 1 - ahead)):
            for h in range(2):
                rows_s = pl.ds(pl.multiple_of(h * ROWS + half * HALF, HALF), HALF)
                outs[part][at, h * 128 : (h + 1) * 128] = acc[rows_s, :]
                outs[2 + part][at, h * 128 : (h + 1) * 128] = l_s[rows_s, :]
        return carry

    lax.fori_loop(0, 1 if alone else 3, q_block, 0)


def far_kernel(ahead, info_ref, ends_ref, lo_ref, hi_ref, flag_in, q_ref, mine_ref, other_ref, acc_in, l_in, acc_one, l_one, *refs):
    near_safe = flag_in[0] == 1
    if ahead:
        out_ref, flag_ref, q_s, acc, m_s, l_s, start_s, keep_s = refs
        safe = near_safe & no_reference_needed(q_ref, mine_ref, other_ref)
        flag_ref[0] = jnp.where(near_safe, 1, 0)
        flag_ref[1] = jnp.where(safe, 1, 0)
        half = info_ref[6]
    else:
        out_ref, q_s, acc, m_s, l_s, start_s, keep_s = refs
        safe = flag_in[1] == 1
        half = 1 - info_ref[6]

    def q_block(plane, carry):
        gq = (plane * 8 + info_ref[4]) * 2 + half
        rows = pl.ds(pl.multiple_of(plane * ROWS + half * HALF, HALF), HALF)
        at = pl.ds(pl.multiple_of(plane * HALF, HALF), HALF)
        for h in range(2):
            part, cols = slice(h * HALF, (h + 1) * HALF), slice(h * 128, (h + 1) * 128)
            q_s[part, :] = q_ref[rows, cols]

        stored = pl.ds(pl.multiple_of((plane - jnp.minimum(plane, 1)) * HALF, HALF), HALF)

        def load(keep):
            def put(acc_from, l_from, rows_from):
                for h in range(2):
                    part, cols = slice(h * HALF, (h + 1) * HALF), slice(h * 128, (h + 1) * 128)
                    before, sums = acc_from[rows_from, cols], l_from[rows_from, cols]
                    if keep is not None:
                        kept = keep[part, :] > 0.0
                        before = jnp.where(kept, acc[part, :], before)
                        sums = jnp.where(kept, l_s[part, :], sums)
                    acc[part, :] = before
                    l_s[part, :] = sums

            @pl.when(plane == 1)
            def _():
                put(acc_one, l_one, slice(None))

            @pl.when(plane != 1)
            def _():
                put(acc_in, l_in, stored)

        load(None)

        @pl.when(jnp.logical_not(safe))
        def _():
            lane = lax.broadcasted_iota(jnp.int32, l_s.shape, 1)
            old = l_s[...]
            total = jnp.sum(old, axis=1, keepdims=True)
            row_sum = jnp.where(near_safe, total, old[:, :1])
            reference = jnp.where(near_safe, jnp.where(total > 0.0, 0.0, NEG), old[:, 64:65])
            l_s[...] = jnp.where(lane == 0, row_sum, 0.0)
            m_s[...] = jnp.broadcast_to(reference, m_s.shape)

        undo = load
        attend_blocks(
            HALF, gq * HALF, info_ref, ends_ref, lo_ref[gq], hi_ref[gq], safe,
            mine_ref, other_ref, q_s, acc, m_s, l_s, start_s, keep_s, undo,
        )
        for h in range(2):
            part, cols = slice(h * HALF, (h + 1) * HALF), slice(h * 128, (h + 1) * 128)
            total = jnp.sum(l_s[part, :], axis=1, keepdims=True)
            out_ref[at, cols] = (acc[part, :] / total).astype(jnp.bfloat16)
        return carry

    lax.fori_loop(0, 4, q_block, 0)


def kernel_call(kernel, name, share, tile, outs, out_flags, args, scalars):
    whole = pl.BlockSpec(memory_space=pltpu.VMEM)
    scalar = pl.BlockSpec(memory_space=pltpu.SMEM)
    return pl.pallas_call(
        kernel,
        out_shape=outs,
        in_specs=[scalar] * scalars + [whole] * (len(args) - scalars),
        out_specs=tuple(scalar if flag else whole for flag in out_flags),
        scratch_shapes=[pltpu.VMEM((2 * tile, 128), jnp.bfloat16)]
        + [pltpu.VMEM((2 * tile, 128), jnp.float32)] * 3
        + [pltpu.VMEM((tile, 128), jnp.int32), pltpu.VMEM((2 * tile, 128), jnp.float32)],
        compiler_params=pltpu.CompilerParams(vmem_limit_bytes=40 * 1024 * 1024),
        cost_estimate=pl.CostEstimate(
            flops=12_000_000_000 // share, bytes_accessed=8 * 1024 * 1024, transcendentals=12_000_000 // share
        ),
        name=name,
    )(*args)


def pick(stacked, index):
    return lax.dynamic_index_in_dim(stacked, index, 0, keepdims=False)


def on_device(queries, keys, values, doc_lengths, out_weight):
    ctx = lax.axis_index("ctx")
    kv = lax.axis_index("kv")
    z, y_lo, x = ctx // 8, ctx // 4 % 2, ctx % 4
    y_hi, core = kv // 2, kv % 2
    j = ctx % 8
    mine_d = 2 * (z % 2) + core
    ends = jnp.cumsum(doc_lengths).astype(jnp.int32)
    blocks = jnp.arange(64, dtype=jnp.int32) * HALF

    def start_of(position):
        return jnp.max(jnp.where(ends[None, :] <= position[:, None], ends[None, :], 0), axis=1)

    lo, hi = start_of(blocks), start_of(blocks + HALF - 1)

    def kv_piece(d):
        at = (d % 2 * HALF, d // 2 * 128)
        return jnp.concatenate(
            [lax.dynamic_slice(keys, at, (HALF, 128)), lax.dynamic_slice(values, at, (HALF, 128))], axis=1
        )

    def q_piece(d):
        return lax.dynamic_slice(queries, (0, d * 256), (512, 256))

    got = [send(kv_piece(z ^ k), TO_HEAD[k]) for k in range(4)]
    got = jnp.stack(got)
    a0 = jnp.stack([pick(got, mine_d ^ plane) for plane in range(4)])

    b0 = send(a0, Y_LO)
    a1 = send(a0, X_DOWN)
    a3 = send(a0, X_UP)
    q_got = jnp.stack([send(q_piece(z ^ k), TO_HEAD[k]) for k in range(4)])
    q = jnp.concatenate([pick(q_got, mine_d ^ plane) for plane in range(4)], axis=0)
    b0, a1, a3, q = lax.optimization_barrier((b0, a1, a3, q))
    near = jnp.stack([a0, a1, a3, b0])
    near_other = send(near, CORE)
    a2 = send(a1, X_DOWN)
    b3 = send(b0, X_UP)
    b1 = send(a1, Y_LO)
    b2 = send(b0, X_TWO)
    here, there = y_lo * 4, (1 - y_lo) * 4
    near_info = jnp.stack([here + x, here + (x + 1) % 4, here + (x + 3) % 4, there + x, j, core, 1 - y_hi]).astype(jnp.int32)
    far_info = jnp.stack(
        [there + (x + 1) % 4, there + (x + 3) % 4, here + (x + 2) % 4, there + (x + 2) % 4, j, core, 1 - y_hi]
    ).astype(jnp.int32)
    flag = jax.ShapeDtypeStruct((2,), jnp.int32)
    wide = jax.ShapeDtypeStruct((768, 256), jnp.float32)
    less = jax.ShapeDtypeStruct((256, 256), jnp.float32)
    narrow = jax.ShapeDtypeStruct((1024, 256), jnp.bfloat16)
    flags, acc_ahead, acc_own, l_ahead, l_own = kernel_call(
        functools.partial(near_kernel, False), "attend_near", 1, ROWS, (flag, wide, wide, wide, wide), (1, 0, 0, 0, 0),
        (near_info, ends, lo, hi, q, near, near_other), 4,
    )
    b1, b3, a2, b2, flags = lax.optimization_barrier((b1, b3, a2, b2, flags))
    far = jnp.stack([b1, b3, a2, b2])
    far_other = send(far, CORE)
    one_ahead, one_own, sum_ahead, sum_own = kernel_call(
        functools.partial(near_kernel, True), "attend_near_one", 2, ROWS, (less, less, less, less), (0, 0, 0, 0),
        (near_info, ends, lo, hi, flags, q, near, near_other), 5,
    )
    out_ahead, flags = kernel_call(
        functools.partial(far_kernel, True), "attend_ahead", 2, HALF, (narrow, flag), (0, 1),
        (far_info, ends, lo, hi, flags, q, far, far_other, acc_ahead, l_ahead, one_ahead, sum_ahead), 5,
    )

    def send_home(out):
        planes = out.reshape(4, 256, 256)
        return tuple(send(pick(planes, mine_d ^ k), TO_HOME[k]) for k in range(4))

    back_ahead = send_home(out_ahead)
    (out_own,) = kernel_call(
        functools.partial(far_kernel, False), "attend_own", 2, HALF, (narrow,), (0,),
        (far_info, ends, lo, hi, flags, q, far, far_other, acc_own, l_own, one_own, sum_own), 5,
    )
    *back_ahead, out_own = lax.optimization_barrier(back_ahead + (out_own,))

    def partial(back):
        back = jnp.stack(back)
        attended = jnp.concatenate([pick(back, z ^ d) for d in range(4)], axis=1)
        part = jnp.dot(attended, out_weight, preferred_element_type=jnp.float32).astype(jnp.bfloat16)
        part = part.reshape(2, 128, 4096)
        return pick(part, core), send(pick(part, 1 - core), CORE)

    kept, arrived = partial(back_ahead)
    ahead = (kept.astype(jnp.float32) + arrived.astype(jnp.float32)).astype(jnp.bfloat16)
    ahead, out_own = lax.optimization_barrier((ahead, out_own))
    far_sum = send(ahead, Y_HI)

    def own_rows(out):
        return partial(send_home(out))

    def no_rows(out):
        return jnp.zeros((128, 4096), jnp.bfloat16), jnp.zeros((128, 4096), jnp.bfloat16)

    kept, arrived = lax.optimization_barrier(lax.cond(doc_lengths[0] > 0, own_rows, no_rows, out_own))
    total = kept.astype(jnp.float32) + arrived.astype(jnp.float32) + far_sum.astype(jnp.float32)
    return total.astype(jnp.bfloat16)


def solution(mesh):
    return jax.shard_map(
        on_device,
        mesh=mesh,
        in_specs=(P("ctx", "kv"), P("ctx", "kv"), P("ctx", "kv"), P(), P("kv", None)),
        out_specs=P(("ctx", "kv"), None),
        check_vma=False,
    )
```

```python
import functools
import math

import jax
import jax.numpy as jnp
from jax import lax
from jax.experimental import pallas as pl
from jax.experimental.pallas import tpu as pltpu
from jax.sharding import PartitionSpec as P

HEAD_WIDTH = 128
NEG = -1e30
AXES = ("ctx", "kv")
SCALE2 = HEAD_WIDTH ** -0.5 * math.log2(math.e)
HALF = 256
ROWS = 512
SAFE = 60.0 * math.log2(math.e)


def device_at(z, y_hi, y_lo, x, c):
    return ((z % 4) * 8 + y_lo * 4 + x % 4) * 4 + y_hi * 2 + c


def permutation(move):
    pairs = []
    for i in range(128):
        ctx, kv = divmod(i, 4)
        pairs.append((i, device_at(*move(ctx // 8, kv // 2, ctx // 4 % 2, ctx % 4, kv % 2))))
    return pairs


X_UP = permutation(lambda z, yh, yl, x, c: (z, yh, yl, x + 1, c))
X_TWO = permutation(lambda z, yh, yl, x, c: (z, yh, yl, x + 2, c))
X_DOWN = permutation(lambda z, yh, yl, x, c: (z, yh, yl, x + 3, c))
Y_LO = permutation(lambda z, yh, yl, x, c: (z, yh, 1 - yl, x, c))
Y_HI = permutation(lambda z, yh, yl, x, c: (z, 1 - yh, yl, x, c))
CORE = permutation(lambda z, yh, yl, x, c: (z, yh, yl, x, 1 - c))
TO_HEAD = [
    permutation(lambda z, yh, yl, x, c, k=k: (2 * c + (z ^ k) // 2, yh, yl, x, (z ^ k) % 2))
    for k in range(4)
]
TO_HOME = [[(b, a) for a, b in pairs] for pairs in TO_HEAD]


def send(x, pairs):
    return lax.ppermute(x, AXES, pairs)


def dot_nt(a, b):
    return lax.dot_general(a, b, (((1,), (1,)), ((), ())), preferred_element_type=jnp.float32)


def fold(p):
    total = p[:, :128]
    for at in range(128, p.shape[1], 128):
        total += p[:, at : at + 128]
    return total


def no_reference_needed(q_ref, mine_ref, other_ref):
    ones = jnp.ones((128, 128), jnp.bfloat16)

    def top_square(block):
        return jnp.max(jnp.dot(block * block, ones, preferred_element_type=jnp.float32), axis=0, keepdims=True)

    def k_top(i, top):
        a = top_square(mine_ref[i, :, :, :128].reshape(1024, 128))
        b = top_square(other_ref[i, :, :, :128].reshape(1024, 128))
        return jnp.maximum(top, jnp.maximum(a, b))

    def q_top(i, top):
        rows = pl.ds(pl.multiple_of(i * ROWS, ROWS), ROWS)
        return jnp.maximum(top, jnp.maximum(top_square(q_ref[rows, :128]), top_square(q_ref[rows, 128:])))

    zero = jnp.zeros((1, 128), jnp.float32)
    bound = lax.fori_loop(0, 4, k_top, zero) * lax.fori_loop(0, 4, q_top, zero)
    return jnp.max(bound) * 1.02 * SCALE2 * SCALE2 <= SAFE * SAFE


def attend_blocks(tile, first_pos, info_ref, ends_ref, lo, hi, safe, mine_ref, other_ref, q_s, acc, m_s, l_s, start_s, keep_s, undo):
    core = info_ref[5]

    @pl.when(lo == hi)
    def _():
        start_s[...] = jnp.full_like(start_s, lo)
        keep_s[...] = jnp.ones_like(keep_s)

    @pl.when(lo != hi)
    def _():
        q_pos = first_pos + lax.broadcasted_iota(jnp.int32, (tile, 128), 0)
        start = jnp.zeros((tile, 128), jnp.int32)
        for doc in range(16):
            end = ends_ref[doc]
            start = jnp.maximum(start, jnp.where(q_pos >= end, end, 0))
        start_s[...] = start
        keep = jnp.where(start <= lo, 1.0, 0.0)
        keep_s[...] = jnp.concatenate([keep, keep], axis=0)

    def keys_values(slot, zk):
        k_all = jnp.concatenate([mine_ref[slot, zk, :, :128], other_ref[slot, zk, :, :128]], axis=0)
        v_all = jnp.concatenate([mine_ref[slot, zk, :, 128:], other_ref[slot, zk, :, 128:]], axis=0)
        return k_all, v_all

    def mask_of(gk):
        column = lax.broadcasted_iota(jnp.int32, (tile, 512), 1)
        k_pos = gk * 512 + jnp.where(core == 0, column, column ^ 256)
        q_at = first_pos + lax.broadcasted_iota(jnp.int32, (tile, 512), 0)
        return (k_pos <= q_at) & (k_pos >= start_s[:, :1])

    parts = [slice(0, tile), slice(tile, 2 * tile)] if tile == ROWS else [slice(0, 2 * tile)]

    def quick(slot, zk, gk, masked):
        k_all, v_all = keys_values(slot, zk)
        if masked:
            allowed = mask_of(gk)
            if tile < ROWS:
                allowed = jnp.concatenate([allowed, allowed], axis=0)
        for part in parts:
            p = jnp.exp2(dot_nt(q_s[part, :], k_all) * SCALE2)
            if masked:
                p = jnp.where(allowed, p, 0.0)
            l_s[part, :] += fold(p)
            acc[part, :] += jnp.dot(p.astype(jnp.bfloat16), v_all, preferred_element_type=jnp.float32)

    def quick_many(blocks):
        pairs = [keys_values(slot, zk) for slot, zk in blocks]
        scores = [[dot_nt(q_s[part, :], k) for k, _ in pairs] for part in parts]
        for part, group in zip(parts, scores):
            total = blend = None
            for s, (_, v) in zip(group, pairs):
                p = jnp.exp2(s * SCALE2)
                sums = fold(p)
                product = jnp.dot(p.astype(jnp.bfloat16), v, preferred_element_type=jnp.float32)
                total = sums if total is None else total + sums
                blend = product if blend is None else blend + product
            l_s[part, :] += total
            acc[part, :] += blend

    def careful(slot, zk, gk):
        k_all, v_all = keys_values(slot, zk)
        allowed = mask_of(gk)
        for h in range(2):
            part = slice(h * tile, (h + 1) * tile)
            s = jnp.where(allowed, dot_nt(q_s[part, :], k_all), NEG)
            m_old = m_s[part, :]
            m_new = jnp.maximum(m_old, jnp.max(s, axis=1, keepdims=True))
            shrink = jnp.exp2((m_old - m_new) * SCALE2)
            p = jnp.where(allowed, jnp.exp2((s - m_new[:, :1]) * SCALE2), 0.0)
            m_s[part, :] = m_new
            l_s[part, :] = l_s[part, :] * shrink + fold(p)
            acc[part, :] = acc[part, :] * shrink + jnp.dot(
                p.astype(jnp.bfloat16), v_all, preferred_element_type=jnp.float32
            )

    def classify(kb):
        slot = kb // 4
        zk = kb % 4
        gk = zk * 8 + info_ref[slot]
        needed = (gk * 512 <= first_pos + tile - 1) & (gk * 512 + 511 >= lo)
        full = (gk * 512 + 511 < first_pos) & (gk * 512 >= lo)
        return slot, zk, gk, needed, full

    def whole_pair(i, carry):
        kb = i // 4 * 8 + i % 4
        a, b = classify(kb), classify(kb + 4)

        @pl.when(a[4] & b[4])
        def _():
            quick_many([a[:2], b[:2]])

        @pl.when(a[4] & jnp.logical_not(b[4]))
        def _():
            quick(*a[:3], False)

        @pl.when(b[4] & jnp.logical_not(a[4]))
        def _():
            quick(*b[:3], False)

        return carry

    def whole_plane(zk, carry):
        four = [classify(4 * slot + zk) for slot in range(4)]
        every = four[0][4] & four[1][4] & four[2][4] & four[3][4]

        @pl.when(every)
        def _():
            quick_many([block[:2] for block in four])

        @pl.when(jnp.logical_not(every))
        def _():
            lax.fori_loop(0, 2, lambda t, c: whole_pair(4 * t + zk, c), 0)

        return carry

    def edge(i, carry):
        diagonal, begin = first_pos // 512, lo // 512
        gk = jnp.where(i == 0, diagonal, begin)
        slot = jnp.int32(4)
        for at in range(4):
            slot = jnp.where(info_ref[at] == gk % 8, at, slot)
        due = (i == 0) | ((begin != diagonal) & (lo % 512 != 0))

        @pl.when(due & (slot < 4))
        def _():
            quick(slot, gk // 8, gk, True)

        return carry

    def any_block(kb, carry):
        slot, zk, gk, needed, _ = classify(kb)

        @pl.when(needed)
        def _():
            careful(slot, zk, gk)

        return carry

    @pl.when(safe)
    def _():
        lax.fori_loop(0, 4, whole_plane, 0)

        @pl.when(lo != hi)
        def _():
            undo(keep_s)

        lax.fori_loop(0, 2, edge, 0)

    @pl.when(jnp.logical_not(safe))
    def _():
        lax.fori_loop(0, 16, any_block, 0)


def near_kernel(alone, info_ref, ends_ref, lo_ref, hi_ref, *refs):
    if alone:
        flag_in, q_ref, mine_ref, other_ref, *refs = refs
        safe = flag_in[0] == 1
    else:
        q_ref, mine_ref, other_ref, flag_ref, *refs = refs
        safe = no_reference_needed(q_ref, mine_ref, other_ref)
        flag_ref[0] = jnp.where(safe, 1, 0)
    refs = tuple(refs)
    outs, (q_s, acc, m_s, l_s, start_s, keep_s) = refs[:4], refs[4:]
    ahead = info_ref[6]

    def q_block(i, carry):
        plane = 1 if alone else i + jnp.minimum(i, 1)
        gq = (plane * 8 + info_ref[4]) * 2
        rows = pl.ds(pl.multiple_of(plane * ROWS, ROWS), ROWS)
        for h in range(2):
            q_s[h * ROWS : (h + 1) * ROWS, :] = q_ref[rows, h * 128 : (h + 1) * 128]
        acc[...] = jnp.zeros_like(acc)
        m_s[...] = jnp.full_like(m_s, NEG)
        l_s[...] = jnp.zeros_like(l_s)

        def undo(keep):
            acc[...] = acc[...] * keep[...]
            l_s[...] = l_s[...] * keep[...]

        attend_blocks(
            ROWS, gq * HALF, info_ref, ends_ref, lo_ref[gq], hi_ref[gq + 1], safe,
            mine_ref, other_ref, q_s, acc, m_s, l_s, start_s, keep_s, undo,
        )

        @pl.when(jnp.logical_not(safe))
        def _():
            lane = lax.broadcasted_iota(jnp.int32, l_s.shape, 1)
            l_s[...] = jnp.where(lane < 64, jnp.sum(l_s[...], axis=1, keepdims=True), m_s[...])

        at = pl.ds(pl.multiple_of(i * HALF, HALF), HALF)
        for part, half in ((0, ahead), (1, 1 - ahead)):
            for h in range(2):
                rows_s = pl.ds(pl.multiple_of(h * ROWS + half * HALF, HALF), HALF)
                outs[part][at, h * 128 : (h + 1) * 128] = acc[rows_s, :]
                outs[2 + part][at, h * 128 : (h + 1) * 128] = l_s[rows_s, :]
        return carry

    lax.fori_loop(0, 1 if alone else 3, q_block, 0)


def far_kernel(ahead, info_ref, ends_ref, lo_ref, hi_ref, flag_in, q_ref, mine_ref, other_ref, acc_in, l_in, acc_one, l_one, *refs):
    near_safe = flag_in[0] == 1
    if ahead:
        out_ref, flag_ref, q_s, acc, m_s, l_s, start_s, keep_s = refs
        safe = near_safe & no_reference_needed(q_ref, mine_ref, other_ref)
        flag_ref[0] = jnp.where(near_safe, 1, 0)
        flag_ref[1] = jnp.where(safe, 1, 0)
        half = info_ref[6]
    else:
        out_ref, q_s, acc, m_s, l_s, start_s, keep_s = refs
        safe = flag_in[1] == 1
        half = 1 - info_ref[6]

    def q_block(plane, carry):
        gq = (plane * 8 + info_ref[4]) * 2 + half
        rows = pl.ds(pl.multiple_of(plane * ROWS + half * HALF, HALF), HALF)
        at = pl.ds(pl.multiple_of(plane * HALF, HALF), HALF)
        for h in range(2):
            part, cols = slice(h * HALF, (h + 1) * HALF), slice(h * 128, (h + 1) * 128)
            q_s[part, :] = q_ref[rows, cols]

        stored = pl.ds(pl.multiple_of((plane - jnp.minimum(plane, 1)) * HALF, HALF), HALF)

        def load(keep):
            def put(acc_from, l_from, rows_from):
                for h in range(2):
                    part, cols = slice(h * HALF, (h + 1) * HALF), slice(h * 128, (h + 1) * 128)
                    before, sums = acc_from[rows_from, cols], l_from[rows_from, cols]
                    if keep is not None:
                        kept = keep[part, :] > 0.0
                        before = jnp.where(kept, acc[part, :], before)
                        sums = jnp.where(kept, l_s[part, :], sums)
                    acc[part, :] = before
                    l_s[part, :] = sums

            @pl.when(plane == 1)
            def _():
                put(acc_one, l_one, slice(None))

            @pl.when(plane != 1)
            def _():
                put(acc_in, l_in, stored)

        load(None)

        @pl.when(jnp.logical_not(safe))
        def _():
            lane = lax.broadcasted_iota(jnp.int32, l_s.shape, 1)
            old = l_s[...]
            total = jnp.sum(old, axis=1, keepdims=True)
            row_sum = jnp.where(near_safe, total, old[:, :1])
            reference = jnp.where(near_safe, jnp.where(total > 0.0, 0.0, NEG), old[:, 64:65])
            l_s[...] = jnp.where(lane == 0, row_sum, 0.0)
            m_s[...] = jnp.broadcast_to(reference, m_s.shape)

        undo = load
        attend_blocks(
            HALF, gq * HALF, info_ref, ends_ref, lo_ref[gq], hi_ref[gq], safe,
            mine_ref, other_ref, q_s, acc, m_s, l_s, start_s, keep_s, undo,
        )
        for h in range(2):
            part, cols = slice(h * HALF, (h + 1) * HALF), slice(h * 128, (h + 1) * 128)
            total = jnp.sum(l_s[part, :], axis=1, keepdims=True)
            out_ref[at, cols] = (acc[part, :] / total).astype(jnp.bfloat16)
        return carry

    lax.fori_loop(0, 4, q_block, 0)


def kernel_call(kernel, name, share, tile, outs, out_flags, args, scalars):
    whole = pl.BlockSpec(memory_space=pltpu.VMEM)
    scalar = pl.BlockSpec(memory_space=pltpu.SMEM)
    return pl.pallas_call(
        kernel,
        out_shape=outs,
        in_specs=[scalar] * scalars + [whole] * (len(args) - scalars),
        out_specs=tuple(scalar if flag else whole for flag in out_flags),
        scratch_shapes=[pltpu.VMEM((2 * tile, 128), jnp.bfloat16)]
        + [pltpu.VMEM((2 * tile, 128), jnp.float32)] * 3
        + [pltpu.VMEM((tile, 128), jnp.int32), pltpu.VMEM((2 * tile, 128), jnp.float32)],
        compiler_params=pltpu.CompilerParams(vmem_limit_bytes=40 * 1024 * 1024),
        cost_estimate=pl.CostEstimate(
            flops=12_000_000_000 // share, bytes_accessed=8 * 1024 * 1024, transcendentals=12_000_000 // share
        ),
        name=name,
    )(*args)


def pick(stacked, index):
    return lax.dynamic_index_in_dim(stacked, index, 0, keepdims=False)


def on_device(queries, keys, values, doc_lengths, out_weight):
    ctx = lax.axis_index("ctx")
    kv = lax.axis_index("kv")
    z, y_lo, x = ctx // 8, ctx // 4 % 2, ctx % 4
    y_hi, core = kv // 2, kv % 2
    j = ctx % 8
    mine_d = 2 * (z % 2) + core
    ends = jnp.cumsum(doc_lengths).astype(jnp.int32)
    blocks = jnp.arange(64, dtype=jnp.int32) * HALF

    def start_of(position):
        return jnp.max(jnp.where(ends[None, :] <= position[:, None], ends[None, :], 0), axis=1)

    lo, hi = start_of(blocks), start_of(blocks + HALF - 1)

    def kv_piece(d):
        at = (d % 2 * HALF, d // 2 * 128)
        return jnp.concatenate(
            [lax.dynamic_slice(keys, at, (HALF, 128)), lax.dynamic_slice(values, at, (HALF, 128))], axis=1
        )

    def q_piece(d):
        return lax.dynamic_slice(queries, (0, d * 256), (512, 256))

    got = [send(kv_piece(z ^ k), TO_HEAD[k]) for k in range(4)]
    got = jnp.stack(got)
    a0 = jnp.stack([pick(got, mine_d ^ plane) for plane in range(4)])

    b0 = send(a0, Y_LO)
    a1 = send(a0, X_DOWN)
    a3 = send(a0, X_UP)
    q_got = jnp.stack([send(q_piece(z ^ k), TO_HEAD[k]) for k in range(4)])
    q = jnp.concatenate([pick(q_got, mine_d ^ plane) for plane in range(4)], axis=0)
    b0, a1, a3, q = lax.optimization_barrier((b0, a1, a3, q))
    near = jnp.stack([a0, a1, a3, b0])
    near_other = send(near, CORE)
    a2 = send(a1, X_DOWN)
    b3 = send(b0, X_UP)
    b1 = send(a1, Y_LO)
    b2 = send(b0, X_TWO)
    here, there = y_lo * 4, (1 - y_lo) * 4
    near_info = jnp.stack([here + x, here + (x + 1) % 4, here + (x + 3) % 4, there + x, j, core, 1 - y_hi]).astype(jnp.int32)
    far_info = jnp.stack(
        [there + (x + 1) % 4, there + (x + 3) % 4, here + (x + 2) % 4, there + (x + 2) % 4, j, core, 1 - y_hi]
    ).astype(jnp.int32)
    flag = jax.ShapeDtypeStruct((2,), jnp.int32)
    wide = jax.ShapeDtypeStruct((768, 256), jnp.float32)
    less = jax.ShapeDtypeStruct((256, 256), jnp.float32)
    narrow = jax.ShapeDtypeStruct((1024, 256), jnp.bfloat16)
    flags, acc_ahead, acc_own, l_ahead, l_own = kernel_call(
        functools.partial(near_kernel, False), "attend_near", 1, ROWS, (flag, wide, wide, wide, wide), (1, 0, 0, 0, 0),
        (near_info, ends, lo, hi, q, near, near_other), 4,
    )
    b1, b3, a2, b2, flags = lax.optimization_barrier((b1, b3, a2, b2, flags))
    far = jnp.stack([b1, b3, a2, b2])
    far_other = send(far, CORE)
    one_ahead, one_own, sum_ahead, sum_own = kernel_call(
        functools.partial(near_kernel, True), "attend_near_one", 2, ROWS, (less, less, less, less), (0, 0, 0, 0),
        (near_info, ends, lo, hi, flags, q, near, near_other), 5,
    )
    out_ahead, flags = kernel_call(
        functools.partial(far_kernel, True), "attend_ahead", 2, HALF, (narrow, flag), (0, 1),
        (far_info, ends, lo, hi, flags, q, far, far_other, acc_ahead, l_ahead, one_ahead, sum_ahead), 5,
    )

    def send_home(out):
        planes = out.reshape(4, 256, 256)
        return tuple(send(pick(planes, mine_d ^ k), TO_HOME[k]) for k in range(4))

    back_ahead = send_home(out_ahead)
    (out_own,) = kernel_call(
        functools.partial(far_kernel, False), "attend_own", 2, HALF, (narrow,), (0,),
        (far_info, ends, lo, hi, flags, q, far, far_other, acc_own, l_own, one_own, sum_own), 5,
    )
    *back_ahead, out_own = lax.optimization_barrier(back_ahead + (out_own,))

    def partial(back):
        back = jnp.stack(back)
        attended = jnp.concatenate([pick(back, z ^ d) for d in range(4)], axis=1)
        part = jnp.dot(attended, out_weight, preferred_element_type=jnp.float32).astype(jnp.bfloat16)
        part = part.reshape(2, 128, 4096)
        return pick(part, core), send(pick(part, 1 - core), CORE)

    kept, arrived = partial(back_ahead)
    ahead = (kept.astype(jnp.float32) + arrived.astype(jnp.float32)).astype(jnp.bfloat16)
    ahead, out_own = lax.optimization_barrier((ahead, out_own))
    far_sum = send(ahead, Y_HI)

    def own_rows(out):
        return partial(send_home(out))

    def no_rows(out):
        return jnp.zeros((128, 4096), jnp.bfloat16), jnp.zeros((128, 4096), jnp.bfloat16)

    kept, arrived = lax.optimization_barrier(lax.cond(doc_lengths[0] > 0, own_rows, no_rows, out_own))
    total = kept.astype(jnp.float32) + arrived.astype(jnp.float32) + far_sum.astype(jnp.float32)
    return total.astype(jnp.bfloat16)


def solution(mesh):
    return jax.shard_map(
        on_device,
        mesh=mesh,
        in_specs=(P("ctx", "kv"), P("ctx", "kv"), P("ctx", "kv"), P(), P("kv", None)),
        out_specs=P(("ctx", "kv"), None),
        check_vma=False,
    )
```

```python
import functools
import math

import jax
import jax.numpy as jnp
from jax import lax
from jax.experimental import pallas as pl
from jax.experimental.pallas import tpu as pltpu
from jax.sharding import PartitionSpec as P

HEAD_WIDTH = 128
NEG = -1e30
AXES = ("ctx", "kv")
SCALE2 = HEAD_WIDTH ** -0.5 * math.log2(math.e)
HALF = 256
ROWS = 512
SAFE = 60.0 * math.log2(math.e)


def device_at(z, y_hi, y_lo, x, c):
    return ((z % 4) * 8 + y_lo * 4 + x % 4) * 4 + y_hi * 2 + c


def permutation(move):
    pairs = []
    for i in range(128):
        ctx, kv = divmod(i, 4)
        pairs.append((i, device_at(*move(ctx // 8, kv // 2, ctx // 4 % 2, ctx % 4, kv % 2))))
    return pairs


X_UP = permutation(lambda z, yh, yl, x, c: (z, yh, yl, x + 1, c))
X_TWO = permutation(lambda z, yh, yl, x, c: (z, yh, yl, x + 2, c))
X_DOWN = permutation(lambda z, yh, yl, x, c: (z, yh, yl, x + 3, c))
Y_LO = permutation(lambda z, yh, yl, x, c: (z, yh, 1 - yl, x, c))
Y_HI = permutation(lambda z, yh, yl, x, c: (z, 1 - yh, yl, x, c))
CORE = permutation(lambda z, yh, yl, x, c: (z, yh, yl, x, 1 - c))
TO_HEAD = [
    permutation(lambda z, yh, yl, x, c, k=k: (2 * c + (z ^ k) // 2, yh, yl, x, (z ^ k) % 2))
    for k in range(4)
]
TO_HOME = [[(b, a) for a, b in pairs] for pairs in TO_HEAD]


def send(x, pairs):
    return lax.ppermute(x, AXES, pairs)


def dot_nt(a, b):
    return lax.dot_general(a, b, (((1,), (1,)), ((), ())), preferred_element_type=jnp.float32)


def fold(p):
    total = p[:, :128]
    for at in range(128, p.shape[1], 128):
        total += p[:, at : at + 128]
    return total


def no_reference_needed(q_ref, mine_ref, other_ref):
    ones = jnp.ones((128, 128), jnp.bfloat16)

    def top_square(block):
        return jnp.max(jnp.dot(block * block, ones, preferred_element_type=jnp.float32), axis=0, keepdims=True)

    def k_top(i, top):
        a = top_square(mine_ref[i, :, :, :128].reshape(1024, 128))
        b = top_square(other_ref[i, :, :, :128].reshape(1024, 128))
        return jnp.maximum(top, jnp.maximum(a, b))

    def q_top(i, top):
        rows = pl.ds(pl.multiple_of(i * ROWS, ROWS), ROWS)
        return jnp.maximum(top, jnp.maximum(top_square(q_ref[rows, :128]), top_square(q_ref[rows, 128:])))

    zero = jnp.zeros((1, 128), jnp.float32)
    bound = lax.fori_loop(0, 4, k_top, zero) * lax.fori_loop(0, 4, q_top, zero)
    return jnp.max(bound) * 1.02 * SCALE2 * SCALE2 <= SAFE * SAFE


def attend_blocks(tile, first_pos, info_ref, ends_ref, lo, hi, safe, mine_ref, other_ref, q_s, acc, m_s, l_s, start_s, keep_s, undo):
    core = info_ref[5]

    @pl.when(lo == hi)
    def _():
        start_s[...] = jnp.full_like(start_s, lo)
        keep_s[...] = jnp.ones_like(keep_s)

    @pl.when(lo != hi)
    def _():
        q_pos = first_pos + lax.broadcasted_iota(jnp.int32, (tile, 128), 0)
        start = jnp.zeros((tile, 128), jnp.int32)
        for doc in range(16):
            end = ends_ref[doc]
            start = jnp.maximum(start, jnp.where(q_pos >= end, end, 0))
        start_s[...] = start
        keep = jnp.where(start <= lo, 1.0, 0.0)
        keep_s[...] = jnp.concatenate([keep, keep], axis=0)

    def keys_values(slot, zk):
        k_all = jnp.concatenate([mine_ref[slot, zk, :, :128], other_ref[slot, zk, :, :128]], axis=0)
        v_all = jnp.concatenate([mine_ref[slot, zk, :, 128:], other_ref[slot, zk, :, 128:]], axis=0)
        return k_all, v_all

    def mask_of(gk):
        column = lax.broadcasted_iota(jnp.int32, (tile, 512), 1)
        k_pos = gk * 512 + jnp.where(core == 0, column, column ^ 256)
        q_at = first_pos + lax.broadcasted_iota(jnp.int32, (tile, 512), 0)
        return (k_pos <= q_at) & (k_pos >= start_s[:, :1])

    parts = [slice(0, tile), slice(tile, 2 * tile)] if tile == ROWS else [slice(0, 2 * tile)]

    def quick(slot, zk, gk, masked):
        k_all, v_all = keys_values(slot, zk)
        if masked:
            allowed = mask_of(gk)
            if tile < ROWS:
                allowed = jnp.concatenate([allowed, allowed], axis=0)
        for part in parts:
            p = jnp.exp2(dot_nt(q_s[part, :], k_all) * SCALE2)
            if masked:
                p = jnp.where(allowed, p, 0.0)
            l_s[part, :] += fold(p)
            acc[part, :] += jnp.dot(p.astype(jnp.bfloat16), v_all, preferred_element_type=jnp.float32)

    def quick_many(blocks):
        pairs = [keys_values(slot, zk) for slot, zk in blocks]
        scores = [[dot_nt(q_s[part, :], k) for k, _ in pairs] for part in parts]
        for part, group in zip(parts, scores):
            total = blend = None
            for s, (_, v) in zip(group, pairs):
                p = jnp.exp2(s * SCALE2)
                sums = fold(p)
                product = jnp.dot(p.astype(jnp.bfloat16), v, preferred_element_type=jnp.float32)
                total = sums if total is None else total + sums
                blend = product if blend is None else blend + product
            l_s[part, :] += total
            acc[part, :] += blend

    def careful(slot, zk, gk):
        k_all, v_all = keys_values(slot, zk)
        allowed = mask_of(gk)

        def head(h, carry):
            part = pl.ds(pl.multiple_of(h * tile, tile), tile)
            s = jnp.where(allowed, dot_nt(q_s[part, :], k_all), NEG)
            m_old = m_s[part, :]
            m_new = jnp.maximum(m_old, jnp.max(s, axis=1, keepdims=True))
            shrink = jnp.exp2((m_old - m_new) * SCALE2)
            p = jnp.where(allowed, jnp.exp2((s - m_new[:, :1]) * SCALE2), 0.0)
            m_s[part, :] = m_new
            l_s[part, :] = l_s[part, :] * shrink + fold(p)
            acc[part, :] = acc[part, :] * shrink + jnp.dot(
                p.astype(jnp.bfloat16), v_all, preferred_element_type=jnp.float32
            )
            return carry

        lax.fori_loop(0, 2, head, 0)

    def classify(kb):
        slot = kb // 4
        zk = kb % 4
        gk = zk * 8 + info_ref[slot]
        needed = (gk * 512 <= first_pos + tile - 1) & (gk * 512 + 511 >= lo)
        full = (gk * 512 + 511 < first_pos) & (gk * 512 >= lo)
        return slot, zk, gk, needed, full

    def whole_block(kb, carry):
        slot, zk, gk, _, full = classify(kb)

        @pl.when(full)
        def _():
            quick(slot, zk, gk, False)

        return carry

    def whole_plane(zk, carry):
        four = [classify(4 * slot + zk) for slot in range(4)]
        every = four[0][4] & four[1][4] & four[2][4] & four[3][4]

        @pl.when(every)
        def _():
            quick_many([block[:2] for block in four])

        @pl.when(jnp.logical_not(every))
        def _():
            lax.fori_loop(0, 4, lambda slot, c: whole_block(4 * slot + zk, c), 0)

        return carry

    def edge(i, carry):
        diagonal, begin = first_pos // 512, lo // 512
        gk = jnp.where(i == 0, diagonal, begin)
        slot = jnp.int32(4)
        for at in range(4):
            slot = jnp.where(info_ref[at] == gk % 8, at, slot)
        due = (i == 0) | ((begin != diagonal) & (lo % 512 != 0))

        @pl.when(due & (slot < 4))
        def _():
            quick(slot, gk // 8, gk, True)

        return carry

    def any_block(kb, carry):
        slot, zk, gk, needed, _ = classify(kb)

        @pl.when(needed)
        def _():
            careful(slot, zk, gk)

        return carry

    @pl.when(safe)
    def _():
        lax.fori_loop(0, 4, whole_plane, 0)

        @pl.when(lo != hi)
        def _():
            undo(keep_s)

        lax.fori_loop(0, 2, edge, 0)

    @pl.when(jnp.logical_not(safe))
    def _():
        lax.fori_loop(0, 16, any_block, 0)


def near_kernel(alone, info_ref, ends_ref, lo_ref, hi_ref, *refs):
    if alone:
        flag_in, q_ref, mine_ref, other_ref, *refs = refs
        safe = flag_in[0] == 1
    else:
        q_ref, mine_ref, other_ref, flag_ref, *refs = refs
        safe = no_reference_needed(q_ref, mine_ref, other_ref)
        flag_ref[0] = jnp.where(safe, 1, 0)
    refs = tuple(refs)
    outs, (q_s, acc, m_s, l_s, start_s, keep_s) = refs[:4], refs[4:]
    ahead = info_ref[6]

    def q_block(i, carry):
        plane = 1 if alone else i + jnp.minimum(i, 1)
        gq = (plane * 8 + info_ref[4]) * 2
        rows = pl.ds(pl.multiple_of(plane * ROWS, ROWS), ROWS)
        for h in range(2):
            q_s[h * ROWS : (h + 1) * ROWS, :] = q_ref[rows, h * 128 : (h + 1) * 128]
        acc[...] = jnp.zeros_like(acc)
        m_s[...] = jnp.full_like(m_s, NEG)
        l_s[...] = jnp.zeros_like(l_s)

        def undo(keep):
            acc[...] = acc[...] * keep[...]
            l_s[...] = l_s[...] * keep[...]

        attend_blocks(
            ROWS, gq * HALF, info_ref, ends_ref, lo_ref[gq], hi_ref[gq + 1], safe,
            mine_ref, other_ref, q_s, acc, m_s, l_s, start_s, keep_s, undo,
        )

        @pl.when(jnp.logical_not(safe))
        def _():
            lane = lax.broadcasted_iota(jnp.int32, l_s.shape, 1)
            l_s[...] = jnp.where(lane < 64, jnp.sum(l_s[...], axis=1, keepdims=True), m_s[...])

        at = pl.ds(pl.multiple_of(i * HALF, HALF), HALF)
        for part, half in ((0, ahead), (1, 1 - ahead)):
            for h in range(2):
                rows_s = pl.ds(pl.multiple_of(h * ROWS + half * HALF, HALF), HALF)
                outs[part][at, h * 128 : (h + 1) * 128] = acc[rows_s, :]
                outs[2 + part][at, h * 128 : (h + 1) * 128] = l_s[rows_s, :]
        return carry

    lax.fori_loop(0, 1 if alone else 3, q_block, 0)


def far_kernel(ahead, info_ref, ends_ref, lo_ref, hi_ref, flag_in, q_ref, mine_ref, other_ref, acc_in, l_in, acc_one, l_one, *refs):
    near_safe = flag_in[0] == 1
    if ahead:
        out_ref, flag_ref, q_s, acc, m_s, l_s, start_s, keep_s = refs
        safe = near_safe & no_reference_needed(q_ref, mine_ref, other_ref)
        flag_ref[0] = jnp.where(near_safe, 1, 0)
        flag_ref[1] = jnp.where(safe, 1, 0)
        half = info_ref[6]
    else:
        out_ref, q_s, acc, m_s, l_s, start_s, keep_s = refs
        safe = flag_in[1] == 1
        half = 1 - info_ref[6]

    def q_block(plane, carry):
        gq = (plane * 8 + info_ref[4]) * 2 + half
        rows = pl.ds(pl.multiple_of(plane * ROWS + half * HALF, HALF), HALF)
        at = pl.ds(pl.multiple_of(plane * HALF, HALF), HALF)
        for h in range(2):
            part, cols = slice(h * HALF, (h + 1) * HALF), slice(h * 128, (h + 1) * 128)
            q_s[part, :] = q_ref[rows, cols]

        stored = pl.ds(pl.multiple_of((plane - jnp.minimum(plane, 1)) * HALF, HALF), HALF)

        def load(keep):
            def put(acc_from, l_from, rows_from):
                for h in range(2):
                    part, cols = slice(h * HALF, (h + 1) * HALF), slice(h * 128, (h + 1) * 128)
                    before, sums = acc_from[rows_from, cols], l_from[rows_from, cols]
                    if keep is not None:
                        kept = keep[part, :] > 0.0
                        before = jnp.where(kept, acc[part, :], before)
                        sums = jnp.where(kept, l_s[part, :], sums)
                    acc[part, :] = before
                    l_s[part, :] = sums

            @pl.when(plane == 1)
            def _():
                put(acc_one, l_one, slice(None))

            @pl.when(plane != 1)
            def _():
                put(acc_in, l_in, stored)

        load(None)

        @pl.when(jnp.logical_not(safe))
        def _():
            lane = lax.broadcasted_iota(jnp.int32, l_s.shape, 1)
            old = l_s[...]
            total = jnp.sum(old, axis=1, keepdims=True)
            row_sum = jnp.where(near_safe, total, old[:, :1])
            reference = jnp.where(near_safe, jnp.where(total > 0.0, 0.0, NEG), old[:, 64:65])
            l_s[...] = jnp.where(lane == 0, row_sum, 0.0)
            m_s[...] = jnp.broadcast_to(reference, m_s.shape)

        undo = load
        attend_blocks(
            HALF, gq * HALF, info_ref, ends_ref, lo_ref[gq], hi_ref[gq], safe,
            mine_ref, other_ref, q_s, acc, m_s, l_s, start_s, keep_s, undo,
        )
        for h in range(2):
            part, cols = slice(h * HALF, (h + 1) * HALF), slice(h * 128, (h + 1) * 128)
            total = jnp.sum(l_s[part, :], axis=1, keepdims=True)
            out_ref[at, cols] = (acc[part, :] / total).astype(jnp.bfloat16)
        return carry

    lax.fori_loop(0, 4, q_block, 0)


def kernel_call(kernel, name, share, tile, outs, out_flags, args, scalars):
    whole = pl.BlockSpec(memory_space=pltpu.VMEM)
    scalar = pl.BlockSpec(memory_space=pltpu.SMEM)
    return pl.pallas_call(
        kernel,
        out_shape=outs,
        in_specs=[scalar] * scalars + [whole] * (len(args) - scalars),
        out_specs=tuple(scalar if flag else whole for flag in out_flags),
        scratch_shapes=[pltpu.VMEM((2 * tile, 128), jnp.bfloat16)]
        + [pltpu.VMEM((2 * tile, 128), jnp.float32)] * 3
        + [pltpu.VMEM((tile, 128), jnp.int32), pltpu.VMEM((2 * tile, 128), jnp.float32)],
        compiler_params=pltpu.CompilerParams(vmem_limit_bytes=40 * 1024 * 1024),
        cost_estimate=pl.CostEstimate(
            flops=12_000_000_000 // share, bytes_accessed=8 * 1024 * 1024, transcendentals=12_000_000 // share
        ),
        name=name,
    )(*args)


def pick(stacked, index):
    return lax.dynamic_index_in_dim(stacked, index, 0, keepdims=False)


def on_device(queries, keys, values, doc_lengths, out_weight):
    ctx = lax.axis_index("ctx")
    kv = lax.axis_index("kv")
    z, y_lo, x = ctx // 8, ctx // 4 % 2, ctx % 4
    y_hi, core = kv // 2, kv % 2
    j = ctx % 8
    mine_d = 2 * (z % 2) + core
    ends = jnp.cumsum(doc_lengths).astype(jnp.int32)
    blocks = jnp.arange(64, dtype=jnp.int32) * HALF

    def start_of(position):
        return jnp.max(jnp.where(ends[None, :] <= position[:, None], ends[None, :], 0), axis=1)

    lo, hi = start_of(blocks), start_of(blocks + HALF - 1)

    def kv_piece(d):
        at = (d % 2 * HALF, d // 2 * 128)
        return jnp.concatenate(
            [lax.dynamic_slice(keys, at, (HALF, 128)), lax.dynamic_slice(values, at, (HALF, 128))], axis=1
        )

    def q_piece(d):
        return lax.dynamic_slice(queries, (0, d * 256), (512, 256))

    got = [send(kv_piece(z ^ k), TO_HEAD[k]) for k in range(4)]
    got = jnp.stack(got)
    a0 = jnp.stack([pick(got, mine_d ^ plane) for plane in range(4)])

    b0 = send(a0, Y_LO)
    a1 = send(a0, X_DOWN)
    a3 = send(a0, X_UP)
    q_got = jnp.stack([send(q_piece(z ^ k), TO_HEAD[k]) for k in range(4)])
    q = jnp.concatenate([pick(q_got, mine_d ^ plane) for plane in range(4)], axis=0)
    b0, a1, a3, q = lax.optimization_barrier((b0, a1, a3, q))
    near = jnp.stack([a0, a1, a3, b0])
    near_other = send(near, CORE)
    a2 = send(a1, X_DOWN)
    b3 = send(b0, X_UP)
    b1 = send(a1, Y_LO)
    b2 = send(b0, X_TWO)
    here, there = y_lo * 4, (1 - y_lo) * 4
    near_info = jnp.stack([here + x, here + (x + 1) % 4, here + (x + 3) % 4, there + x, j, core, 1 - y_hi]).astype(jnp.int32)
    far_info = jnp.stack(
        [there + (x + 1) % 4, there + (x + 3) % 4, here + (x + 2) % 4, there + (x + 2) % 4, j, core, 1 - y_hi]
    ).astype(jnp.int32)
    flag = jax.ShapeDtypeStruct((2,), jnp.int32)
    wide = jax.ShapeDtypeStruct((768, 256), jnp.float32)
    less = jax.ShapeDtypeStruct((256, 256), jnp.float32)
    narrow = jax.ShapeDtypeStruct((1024, 256), jnp.bfloat16)
    flags, acc_ahead, acc_own, l_ahead, l_own = kernel_call(
        functools.partial(near_kernel, False), "attend_near", 1, ROWS, (flag, wide, wide, wide, wide), (1, 0, 0, 0, 0),
        (near_info, ends, lo, hi, q, near, near_other), 4,
    )
    b1, b3, a2, b2, flags = lax.optimization_barrier((b1, b3, a2, b2, flags))
    far = jnp.stack([b1, b3, a2, b2])
    far_other = send(far, CORE)
    one_ahead, one_own, sum_ahead, sum_own = kernel_call(
        functools.partial(near_kernel, True), "attend_near_one", 2, ROWS, (less, less, less, less), (0, 0, 0, 0),
        (near_info, ends, lo, hi, flags, q, near, near_other), 5,
    )
    out_ahead, flags = kernel_call(
        functools.partial(far_kernel, True), "attend_ahead", 2, HALF, (narrow, flag), (0, 1),
        (far_info, ends, lo, hi, flags, q, far, far_other, acc_ahead, l_ahead, one_ahead, sum_ahead), 5,
    )

    def send_home(out):
        planes = out.reshape(4, 256, 256)
        return tuple(send(pick(planes, mine_d ^ k), TO_HOME[k]) for k in range(4))

    back_ahead = send_home(out_ahead)
    (out_own,) = kernel_call(
        functools.partial(far_kernel, False), "attend_own", 2, HALF, (narrow,), (0,),
        (far_info, ends, lo, hi, flags, q, far, far_other, acc_own, l_own, one_own, sum_own), 5,
    )
    *back_ahead, out_own = lax.optimization_barrier(back_ahead + (out_own,))

    def partial(back):
        back = jnp.stack(back)
        attended = jnp.concatenate([pick(back, z ^ d) for d in range(4)], axis=1)
        part = jnp.dot(attended, out_weight, preferred_element_type=jnp.float32).astype(jnp.bfloat16)
        part = part.reshape(2, 128, 4096)
        return pick(part, core), send(pick(part, 1 - core), CORE)

    kept, arrived = partial(back_ahead)
    ahead = (kept.astype(jnp.float32) + arrived.astype(jnp.float32)).astype(jnp.bfloat16)
    ahead, out_own = lax.optimization_barrier((ahead, out_own))
    far_sum = send(ahead, Y_HI)

    def own_rows(out):
        return partial(send_home(out))

    def no_rows(out):
        return jnp.zeros((128, 4096), jnp.bfloat16), jnp.zeros((128, 4096), jnp.bfloat16)

    kept, arrived = lax.optimization_barrier(lax.cond(doc_lengths[0] > 0, own_rows, no_rows, out_own))
    total = kept.astype(jnp.float32) + arrived.astype(jnp.float32) + far_sum.astype(jnp.float32)
    return total.astype(jnp.bfloat16)


def solution(mesh):
    return jax.shard_map(
        on_device,
        mesh=mesh,
        in_specs=(P("ctx", "kv"), P("ctx", "kv"), P("ctx", "kv"), P(), P("kv", None)),
        out_specs=P(("ctx", "kv"), None),
        check_vma=False,
    )
```

```python
import functools
import math

import jax
import jax.numpy as jnp
from jax import lax
from jax.experimental import pallas as pl
from jax.experimental.pallas import tpu as pltpu
from jax.sharding import PartitionSpec as P

HEAD_WIDTH = 128
NEG = -1e30
AXES = ("ctx", "kv")
SCALE2 = HEAD_WIDTH ** -0.5 * math.log2(math.e)
HALF = 256
ROWS = 512
SAFE = 60.0 * math.log2(math.e)


def device_at(z, y_hi, y_lo, x, c):
    return ((z % 4) * 8 + y_lo * 4 + x % 4) * 4 + y_hi * 2 + c


def permutation(move):
    pairs = []
    for i in range(128):
        ctx, kv = divmod(i, 4)
        pairs.append((i, device_at(*move(ctx // 8, kv // 2, ctx // 4 % 2, ctx % 4, kv % 2))))
    return pairs


X_UP = permutation(lambda z, yh, yl, x, c: (z, yh, yl, x + 1, c))
X_TWO = permutation(lambda z, yh, yl, x, c: (z, yh, yl, x + 2, c))
X_DOWN = permutation(lambda z, yh, yl, x, c: (z, yh, yl, x + 3, c))
Y_LO = permutation(lambda z, yh, yl, x, c: (z, yh, 1 - yl, x, c))
Y_HI = permutation(lambda z, yh, yl, x, c: (z, 1 - yh, yl, x, c))
CORE = permutation(lambda z, yh, yl, x, c: (z, yh, yl, x, 1 - c))
TO_HEAD = [
    permutation(lambda z, yh, yl, x, c, k=k: (2 * c + (z ^ k) // 2, yh, yl, x, (z ^ k) % 2))
    for k in range(4)
]
TO_HOME = [[(b, a) for a, b in pairs] for pairs in TO_HEAD]


def send(x, pairs):
    return lax.ppermute(x, AXES, pairs)


def dot_nt(a, b):
    return lax.dot_general(a, b, (((1,), (1,)), ((), ())), preferred_element_type=jnp.float32)


def fold(p):
    total = p[:, :128]
    for at in range(128, p.shape[1], 128):
        total += p[:, at : at + 128]
    return total


def no_reference_needed(q_ref, mine_ref, other_ref):
    ones = jnp.ones((128, 128), jnp.bfloat16)

    def top_square(block):
        return jnp.max(jnp.dot(block * block, ones, preferred_element_type=jnp.float32), axis=0, keepdims=True)

    def k_top(i, top):
        a = top_square(mine_ref[i, :, :, :128].reshape(1024, 128))
        b = top_square(other_ref[i, :, :, :128].reshape(1024, 128))
        return jnp.maximum(top, jnp.maximum(a, b))

    def q_top(i, top):
        rows = pl.ds(pl.multiple_of(i * ROWS, ROWS), ROWS)
        return jnp.maximum(top, jnp.maximum(top_square(q_ref[rows, :128]), top_square(q_ref[rows, 128:])))

    zero = jnp.zeros((1, 128), jnp.float32)
    bound = lax.fori_loop(0, 4, k_top, zero) * lax.fori_loop(0, 4, q_top, zero)
    return jnp.max(bound) * 1.02 * SCALE2 * SCALE2 <= SAFE * SAFE


def attend_blocks(tile, first_pos, info_ref, ends_ref, lo, hi, safe, mine_ref, other_ref, q_s, acc, m_s, l_s, start_s, keep_s, undo):
    core = info_ref[5]

    @pl.when(lo == hi)
    def _():
        start_s[...] = jnp.full_like(start_s, lo)
        keep_s[...] = jnp.ones_like(keep_s)

    @pl.when(lo != hi)
    def _():
        q_pos = first_pos + lax.broadcasted_iota(jnp.int32, (tile, 128), 0)
        start = jnp.zeros((tile, 128), jnp.int32)
        for doc in range(16):
            end = ends_ref[doc]
            start = jnp.maximum(start, jnp.where(q_pos >= end, end, 0))
        start_s[...] = start
        keep = jnp.where(start <= lo, 1.0, 0.0)
        keep_s[...] = jnp.concatenate([keep, keep], axis=0)

    def keys_values(slot, zk):
        k_all = jnp.concatenate([mine_ref[slot, zk, :, :128], other_ref[slot, zk, :, :128]], axis=0)
        v_all = jnp.concatenate([mine_ref[slot, zk, :, 128:], other_ref[slot, zk, :, 128:]], axis=0)
        return k_all, v_all

    def mask_of(gk):
        column = lax.broadcasted_iota(jnp.int32, (tile, 512), 1)
        k_pos = gk * 512 + jnp.where(core == 0, column, column ^ 256)
        q_at = first_pos + lax.broadcasted_iota(jnp.int32, (tile, 512), 0)
        return (k_pos <= q_at) & (k_pos >= start_s[:, :1])

    parts = [slice(0, tile), slice(tile, 2 * tile)] if tile == ROWS else [slice(0, 2 * tile)]

    def quick(slot, zk, gk, masked):
        k_all, v_all = keys_values(slot, zk)
        if masked:
            allowed = mask_of(gk)
            if tile < ROWS:
                allowed = jnp.concatenate([allowed, allowed], axis=0)
        for part in parts:
            p = jnp.exp2(dot_nt(q_s[part, :], k_all) * SCALE2)
            if masked:
                p = jnp.where(allowed, p, 0.0)
            l_s[part, :] += fold(p)
            acc[part, :] += jnp.dot(p.astype(jnp.bfloat16), v_all, preferred_element_type=jnp.float32)

    def quick_many(blocks):
        pairs = [keys_values(slot, zk) for slot, zk in blocks]
        scores = [[dot_nt(q_s[part, :], k) for k, _ in pairs] for part in parts]
        for part, group in zip(parts, scores):
            total = blend = None
            for s, (_, v) in zip(group, pairs):
                p = jnp.exp2(s * SCALE2)
                sums = fold(p)
                product = jnp.dot(p.astype(jnp.bfloat16), v, preferred_element_type=jnp.float32)
                total = sums if total is None else total + sums
                blend = product if blend is None else blend + product
            l_s[part, :] += total
            acc[part, :] += blend

    def careful(slot, zk, gk):
        k_all, v_all = keys_values(slot, zk)
        allowed = mask_of(gk)

        def head(h, carry):
            part = pl.ds(pl.multiple_of(h * tile, tile), tile)
            s = jnp.where(allowed, dot_nt(q_s[part, :], k_all), NEG)
            m_old = m_s[part, :]
            m_new = jnp.maximum(m_old, jnp.max(s, axis=1, keepdims=True))
            shrink = jnp.exp2((m_old - m_new) * SCALE2)
            p = jnp.where(allowed, jnp.exp2((s - m_new[:, :1]) * SCALE2), 0.0)
            m_s[part, :] = m_new
            l_s[part, :] = l_s[part, :] * shrink + fold(p)
            acc[part, :] = acc[part, :] * shrink + jnp.dot(
                p.astype(jnp.bfloat16), v_all, preferred_element_type=jnp.float32
            )
            return carry

        lax.fori_loop(0, 2, head, 0)

    def classify(kb):
        slot = kb // 4
        zk = kb % 4
        gk = zk * 8 + info_ref[slot]
        needed = (gk * 512 <= first_pos + tile - 1) & (gk * 512 + 511 >= lo)
        full = (gk * 512 + 511 < first_pos) & (gk * 512 >= lo)
        return slot, zk, gk, needed, full

    def whole_pair(i, carry):
        kb = i // 4 * 8 + i % 4
        a, b = classify(kb), classify(kb + 4)

        @pl.when(a[4] & b[4])
        def _():
            quick_many([a[:2], b[:2]])

        @pl.when(a[4] ^ b[4])
        def _():
            quick(jnp.where(a[4], a[0], b[0]), kb % 4, 0, False)

        return carry

    def whole_plane(zk, carry):
        four = [classify(4 * slot + zk) for slot in range(4)]
        every = four[0][4] & four[1][4] & four[2][4] & four[3][4]

        @pl.when(every)
        def _():
            quick_many([block[:2] for block in four])

        @pl.when(jnp.logical_not(every))
        def _():
            lax.fori_loop(0, 2, lambda t, c: whole_pair(4 * t + zk, c), 0)

        return carry

    def edge(i, carry):
        diagonal, begin = first_pos // 512, lo // 512
        gk = jnp.where(i == 0, diagonal, begin)
        slot = jnp.int32(4)
        for at in range(4):
            slot = jnp.where(info_ref[at] == gk % 8, at, slot)
        due = (i == 0) | ((begin != diagonal) & (lo % 512 != 0))

        @pl.when(due & (slot < 4))
        def _():
            quick(slot, gk // 8, gk, True)

        return carry

    def any_block(kb, carry):
        slot, zk, gk, needed, _ = classify(kb)

        @pl.when(needed)
        def _():
            careful(slot, zk, gk)

        return carry

    @pl.when(safe)
    def _():
        lax.fori_loop(0, 4, whole_plane, 0)

        @pl.when(lo != hi)
        def _():
            undo(keep_s)

        lax.fori_loop(0, 2, edge, 0)

    @pl.when(jnp.logical_not(safe))
    def _():
        lax.fori_loop(0, 16, any_block, 0)


def near_kernel(alone, info_ref, ends_ref, lo_ref, hi_ref, *refs):
    if alone:
        flag_in, q_ref, mine_ref, other_ref, *refs = refs
        safe = flag_in[0] == 1
    else:
        q_ref, mine_ref, other_ref, flag_ref, *refs = refs
        safe = no_reference_needed(q_ref, mine_ref, other_ref)
        flag_ref[0] = jnp.where(safe, 1, 0)
    refs = tuple(refs)
    outs, (q_s, acc, m_s, l_s, start_s, keep_s) = refs[:4], refs[4:]
    ahead = info_ref[6]

    def q_block(i, carry):
        plane = 1 if alone else i + jnp.minimum(i, 1)
        gq = (plane * 8 + info_ref[4]) * 2
        rows = pl.ds(pl.multiple_of(plane * ROWS, ROWS), ROWS)
        for h in range(2):
            q_s[h * ROWS : (h + 1) * ROWS, :] = q_ref[rows, h * 128 : (h + 1) * 128]
        acc[...] = jnp.zeros_like(acc)
        m_s[...] = jnp.full_like(m_s, NEG)
        l_s[...] = jnp.zeros_like(l_s)

        def undo(keep):
            acc[...] = acc[...] * keep[...]
            l_s[...] = l_s[...] * keep[...]

        attend_blocks(
            ROWS, gq * HALF, info_ref, ends_ref, lo_ref[gq], hi_ref[gq + 1], safe,
            mine_ref, other_ref, q_s, acc, m_s, l_s, start_s, keep_s, undo,
        )

        @pl.when(jnp.logical_not(safe))
        def _():
            lane = lax.broadcasted_iota(jnp.int32, l_s.shape, 1)
            l_s[...] = jnp.where(lane < 64, jnp.sum(l_s[...], axis=1, keepdims=True), m_s[...])

        at = pl.ds(pl.multiple_of(i * HALF, HALF), HALF)
        for part, half in ((0, ahead), (1, 1 - ahead)):
            for h in range(2):
                rows_s = pl.ds(pl.multiple_of(h * ROWS + half * HALF, HALF), HALF)
                outs[part][at, h * 128 : (h + 1) * 128] = acc[rows_s, :]
                outs[2 + part][at, h * 128 : (h + 1) * 128] = l_s[rows_s, :]
        return carry

    lax.fori_loop(0, 1 if alone else 3, q_block, 0)


def far_kernel(ahead, info_ref, ends_ref, lo_ref, hi_ref, flag_in, q_ref, mine_ref, other_ref, acc_in, l_in, acc_one, l_one, *refs):
    near_safe = flag_in[0] == 1
    if ahead:
        out_ref, flag_ref, q_s, acc, m_s, l_s, start_s, keep_s = refs
        safe = near_safe & no_reference_needed(q_ref, mine_ref, other_ref)
        flag_ref[0] = jnp.where(near_safe, 1, 0)
        flag_ref[1] = jnp.where(safe, 1, 0)
        half = info_ref[6]
    else:
        out_ref, q_s, acc, m_s, l_s, start_s, keep_s = refs
        safe = flag_in[1] == 1
        half = 1 - info_ref[6]

    def q_block(plane, carry):
        gq = (plane * 8 + info_ref[4]) * 2 + half
        rows = pl.ds(pl.multiple_of(plane * ROWS + half * HALF, HALF), HALF)
        at = pl.ds(pl.multiple_of(plane * HALF, HALF), HALF)
        for h in range(2):
            part, cols = slice(h * HALF, (h + 1) * HALF), slice(h * 128, (h + 1) * 128)
            q_s[part, :] = q_ref[rows, cols]

        stored = pl.ds(pl.multiple_of((plane - jnp.minimum(plane, 1)) * HALF, HALF), HALF)

        def load(keep):
            def put(acc_from, l_from, rows_from):
                for h in range(2):
                    part, cols = slice(h * HALF, (h + 1) * HALF), slice(h * 128, (h + 1) * 128)
                    before, sums = acc_from[rows_from, cols], l_from[rows_from, cols]
                    if keep is not None:
                        kept = keep[part, :] > 0.0
                        before = jnp.where(kept, acc[part, :], before)
                        sums = jnp.where(kept, l_s[part, :], sums)
                    acc[part, :] = before
                    l_s[part, :] = sums

            @pl.when(plane == 1)
            def _():
                put(acc_one, l_one, slice(None))

            @pl.when(plane != 1)
            def _():
                put(acc_in, l_in, stored)

        load(None)

        @pl.when(jnp.logical_not(safe))
        def _():
            lane = lax.broadcasted_iota(jnp.int32, l_s.shape, 1)
            old = l_s[...]
            total = jnp.sum(old, axis=1, keepdims=True)
            row_sum = jnp.where(near_safe, total, old[:, :1])
            reference = jnp.where(near_safe, jnp.where(total > 0.0, 0.0, NEG), old[:, 64:65])
            l_s[...] = jnp.where(lane == 0, row_sum, 0.0)
            m_s[...] = jnp.broadcast_to(reference, m_s.shape)

        undo = load
        attend_blocks(
            HALF, gq * HALF, info_ref, ends_ref, lo_ref[gq], hi_ref[gq], safe,
            mine_ref, other_ref, q_s, acc, m_s, l_s, start_s, keep_s, undo,
        )
        for h in range(2):
            part, cols = slice(h * HALF, (h + 1) * HALF), slice(h * 128, (h + 1) * 128)
            total = jnp.sum(l_s[part, :], axis=1, keepdims=True)
            out_ref[at, cols] = (acc[part, :] / total).astype(jnp.bfloat16)
        return carry

    lax.fori_loop(0, 4, q_block, 0)


def kernel_call(kernel, name, share, tile, outs, out_flags, args, scalars):
    whole = pl.BlockSpec(memory_space=pltpu.VMEM)
    scalar = pl.BlockSpec(memory_space=pltpu.SMEM)
    return pl.pallas_call(
        kernel,
        out_shape=outs,
        in_specs=[scalar] * scalars + [whole] * (len(args) - scalars),
        out_specs=tuple(scalar if flag else whole for flag in out_flags),
        scratch_shapes=[pltpu.VMEM((2 * tile, 128), jnp.bfloat16)]
        + [pltpu.VMEM((2 * tile, 128), jnp.float32)] * 3
        + [pltpu.VMEM((tile, 128), jnp.int32), pltpu.VMEM((2 * tile, 128), jnp.float32)],
        compiler_params=pltpu.CompilerParams(vmem_limit_bytes=40 * 1024 * 1024),
        cost_estimate=pl.CostEstimate(
            flops=12_000_000_000 // share, bytes_accessed=8 * 1024 * 1024, transcendentals=12_000_000 // share
        ),
        name=name,
    )(*args)


def pick(stacked, index):
    return lax.dynamic_index_in_dim(stacked, index, 0, keepdims=False)


def on_device(queries, keys, values, doc_lengths, out_weight):
    ctx = lax.axis_index("ctx")
    kv = lax.axis_index("kv")
    z, y_lo, x = ctx // 8, ctx // 4 % 2, ctx % 4
    y_hi, core = kv // 2, kv % 2
    j = ctx % 8
    mine_d = 2 * (z % 2) + core
    ends = jnp.cumsum(doc_lengths).astype(jnp.int32)
    blocks = jnp.arange(64, dtype=jnp.int32) * HALF

    def start_of(position):
        return jnp.max(jnp.where(ends[None, :] <= position[:, None], ends[None, :], 0), axis=1)

    lo, hi = start_of(blocks), start_of(blocks + HALF - 1)

    def kv_piece(d):
        at = (d % 2 * HALF, d // 2 * 128)
        return jnp.concatenate(
            [lax.dynamic_slice(keys, at, (HALF, 128)), lax.dynamic_slice(values, at, (HALF, 128))], axis=1
        )

    def q_piece(d):
        return lax.dynamic_slice(queries, (0, d * 256), (512, 256))

    got = [send(kv_piece(z ^ k), TO_HEAD[k]) for k in range(4)]
    got = jnp.stack(got)
    a0 = jnp.stack([pick(got, mine_d ^ plane) for plane in range(4)])

    b0 = send(a0, Y_LO)
    a1 = send(a0, X_DOWN)
    a3 = send(a0, X_UP)
    q_got = jnp.stack([send(q_piece(z ^ k), TO_HEAD[k]) for k in range(4)])
    q = jnp.concatenate([pick(q_got, mine_d ^ plane) for plane in range(4)], axis=0)
    b0, a1, a3, q = lax.optimization_barrier((b0, a1, a3, q))
    near = jnp.stack([a0, a1, a3, b0])
    near_other = send(near, CORE)
    a2 = send(a1, X_DOWN)
    b3 = send(b0, X_UP)
    b1 = send(a1, Y_LO)
    b2 = send(b0, X_TWO)
    here, there = y_lo * 4, (1 - y_lo) * 4
    near_info = jnp.stack([here + x, here + (x + 1) % 4, here + (x + 3) % 4, there + x, j, core, 1 - y_hi]).astype(jnp.int32)
    far_info = jnp.stack(
        [there + (x + 1) % 4, there + (x + 3) % 4, here + (x + 2) % 4, there + (x + 2) % 4, j, core, 1 - y_hi]
    ).astype(jnp.int32)
    flag = jax.ShapeDtypeStruct((2,), jnp.int32)
    wide = jax.ShapeDtypeStruct((768, 256), jnp.float32)
    less = jax.ShapeDtypeStruct((256, 256), jnp.float32)
    narrow = jax.ShapeDtypeStruct((1024, 256), jnp.bfloat16)
    flags, acc_ahead, acc_own, l_ahead, l_own = kernel_call(
        functools.partial(near_kernel, False), "attend_near", 1, ROWS, (flag, wide, wide, wide, wide), (1, 0, 0, 0, 0),
        (near_info, ends, lo, hi, q, near, near_other), 4,
    )
    b1, b3, a2, b2, flags = lax.optimization_barrier((b1, b3, a2, b2, flags))
    far = jnp.stack([b1, b3, a2, b2])
    far_other = send(far, CORE)
    one_ahead, one_own, sum_ahead, sum_own = kernel_call(
        functools.partial(near_kernel, True), "attend_near_one", 2, ROWS, (less, less, less, less), (0, 0, 0, 0),
        (near_info, ends, lo, hi, flags, q, near, near_other), 5,
    )
    out_ahead, flags = kernel_call(
        functools.partial(far_kernel, True), "attend_ahead", 2, HALF, (narrow, flag), (0, 1),
        (far_info, ends, lo, hi, flags, q, far, far_other, acc_ahead, l_ahead, one_ahead, sum_ahead), 5,
    )

    def send_home(out):
        planes = out.reshape(4, 256, 256)
        return tuple(send(pick(planes, mine_d ^ k), TO_HOME[k]) for k in range(4))

    back_ahead = send_home(out_ahead)
    (out_own,) = kernel_call(
        functools.partial(far_kernel, False), "attend_own", 2, HALF, (narrow,), (0,),
        (far_info, ends, lo, hi, flags, q, far, far_other, acc_own, l_own, one_own, sum_own), 5,
    )
    *back_ahead, out_own = lax.optimization_barrier(back_ahead + (out_own,))

    def partial(back):
        back = jnp.stack(back)
        attended = jnp.concatenate([pick(back, z ^ d) for d in range(4)], axis=1)
        part = jnp.dot(attended, out_weight, preferred_element_type=jnp.float32).astype(jnp.bfloat16)
        part = part.reshape(2, 128, 4096)
        return pick(part, core), send(pick(part, 1 - core), CORE)

    kept, arrived = partial(back_ahead)
    ahead = (kept.astype(jnp.float32) + arrived.astype(jnp.float32)).astype(jnp.bfloat16)
    ahead, out_own = lax.optimization_barrier((ahead, out_own))
    far_sum = send(ahead, Y_HI)

    def own_rows(out):
        return partial(send_home(out))

    def no_rows(out):
        return jnp.zeros((128, 4096), jnp.bfloat16), jnp.zeros((128, 4096), jnp.bfloat16)

    kept, arrived = lax.optimization_barrier(lax.cond(doc_lengths[0] > 0, own_rows, no_rows, out_own))
    total = kept.astype(jnp.float32) + arrived.astype(jnp.float32) + far_sum.astype(jnp.float32)
    return total.astype(jnp.bfloat16)


def solution(mesh):
    return jax.shard_map(
        on_device,
        mesh=mesh,
        in_specs=(P("ctx", "kv"), P("ctx", "kv"), P("ctx", "kv"), P(), P("kv", None)),
        out_specs=P(("ctx", "kv"), None),
        check_vma=False,
    )
```
